32 devices in a mesh: flow: 8 (over y, x, core), cross: 4 (over z).
Axes of the slice: x: 2, y: 2, z: 4, core: 2. Of those that a mesh axis runs over, the one named last changes fastest.
Arguments:
- solid_temp: float32 [8, 2048, 2048], P(None, 'flow', 'cross'), may hold values from 0.5 to 1.5
- conductance: float32 [8, 2048, 2048], P(None, 'flow', 'cross'), may hold values from 0.03 to 0.12
- coolant: float32 [4, 2048, 2048], P(None, 'flow', 'cross'), may hold values from 0 to 1
- power_index: int32 [2048, 2048], P('flow', 'cross'), may hold values from 0 to 15
- power_levels: float32 [16], replicated, may hold values from 0.05 to 0.5
- channel_mask: int32 [4, 2048], P(None, 'cross'), may hold values 0 or 1
- inlet: float32 [4, 2048], P(None, 'cross'), may hold values from 0 to 0.5
- flow_gain: float32 [4, 2048], P(None, 'cross'), may hold values from 2 to 16
Outputs:
- solid_next: float32 [8, 2048, 2048], P(None, 'flow', 'cross')
- coolant_next: float32 [4, 2048, 2048], P(None, 'flow', 'cross')
The draws below stay inside these ranges and needn't reach their ends.
All inputs are finite; a program needn't handle non-finite values. No bound on the sum of `channel_mask` on one device may be relied on, other than what follows from the above.
Results may differ from the reference program's by a relative error of at most 0.000058.
Values sent between devices are 32-bit elements; how exact they have to be, the bound alone decides.
A program may use at most 128 MiB of HBM per device.

```python
import math
import jax
import jax.numpy as jnp

SOLID = 8
CHAN = 4
LEVELS = 16
NX = 2048
NY = 2048


def plant(drawn, stream_key, low, largest):
    spot = [jax.random.randint(jax.random.fold_in(stream_key, axis), (), 0, length) for axis, length in enumerate(drawn.shape)]
    widest = drawn.shape.index(max(drawn.shape))
    beside = spot[:widest] + [(spot[widest] + 1) % drawn.shape[widest]] + spot[widest + 1:]
    return drawn.at[tuple(spot)].set(low).at[tuple(beside)].set(largest)


def steps_of(rng, dims, split, least, top_value):
    def one(position, shards_of):
        heights = jax.random.uniform(jax.random.fold_in(jax.random.fold_in(rng, 6), position), (shards_of,), jnp.float32, least / len(split), top_value / len(split))
        return jnp.repeat(jnp.exp(heights), dims[position] // shards_of).reshape((-1,) + (1,) * (len(dims) - position - 1))

    gain = one(*split[0])
    for cut in split[1:]:
        gain = gain * one(*cut)
    return gain


def setup_inputs(seed: int = 0) -> dict:
    arg_keys = jax.random.split(jax.random.key(seed), 9)
    solid_temp = jnp.clip(0.5 + 1.0 * jax.random.uniform(arg_keys[0], (SOLID, NX, NY), jnp.float32) ** steps_of(arg_keys[0], (SOLID, NX, NY), ((1, 8), (2, 4)), -0.2, 0.2), 0.5, 1.5)
    conductance = jnp.clip(jnp.exp(math.log(0.12) - 1.3862944 * jax.random.uniform(arg_keys[1], (SOLID, NX, NY), jnp.float32) ** steps_of(arg_keys[1], (SOLID, NX, NY), ((1, 8), (2, 4)), -0.2, 0.2)), 0.03, 0.12)
    coolant = jnp.clip(1.0 * jax.random.uniform(arg_keys[2], (CHAN, NX, NY), jnp.float32) ** steps_of(arg_keys[2], (CHAN, NX, NY), ((1, 8), (2, 4)), -0.2, 0.2), 0.0, 1.0)
    power_index = plant(jax.random.randint(arg_keys[3], (NX, NY), 0, LEVELS), jax.random.fold_in(arg_keys[3], 1), 0, LEVELS - 1).astype(jnp.int32)
    power_levels = jnp.clip(jnp.exp(jax.random.uniform(arg_keys[4], (LEVELS,), jnp.float32, math.log(0.05), math.log(0.5))), 0.05, 0.5)
    channel_mask = plant((jax.random.randint(arg_keys[5], (CHAN, NY), 0, 2) < 1).astype(jnp.int32), jax.random.fold_in(arg_keys[5], 1), 0, 1)
    inlet = jnp.clip(0.5 * jax.random.uniform(arg_keys[6], (CHAN, NY), jnp.float32) ** steps_of(arg_keys[6], (CHAN, NY), ((1, 4),), -0.2, 0.2), 0.0, 0.5)
    flow_gain = jnp.clip(jnp.exp(math.log(16.0) - 2.0794415 * jax.random.uniform(arg_keys[7], (CHAN, NY), jnp.float32) ** steps_of(arg_keys[7], (CHAN, NY), ((1, 4),), -0.2, 0.2)), 2.0, 16.0)
    return dict(solid_temp=solid_temp, conductance=conductance, coolant=coolant, power_index=power_index, power_levels=power_levels, channel_mask=channel_mask, inlet=inlet, flow_gain=flow_gain)


def advance(padded, conduct, heating, coolant_now, open_cols):
    center = padded[:, 1:-1, 1:-1]
    lateral = padded[:, 2:, 1:-1] + padded[:, :-2, 1:-1] + padded[:, 1:-1, 2:] + padded[:, 1:-1, :-2]
    upward = center[1:] - center[:-1]
    no_layer = jnp.zeros_like(center[:1])
    vertical = jnp.concatenate([upward, no_layer], axis=0) - jnp.concatenate([no_layer, upward], axis=0)
    chans = coolant_now.shape[0]
    paired = center.reshape(chans, 2, center.shape[1], center.shape[2])
    film_term = 0.08 * open_cols[:, None, None, :] * (coolant_now[:, None] - paired)
    source = jnp.concatenate([heating[None], jnp.zeros_like(center[1:])], axis=0)
    return center + conduct * (lateral - 4.0 * center) + 0.05 * vertical + film_term.reshape(center.shape) + source


def reference(solid_temp, conductance, coolant, power_index, power_levels, channel_mask, inlet, flow_gain):
    heating = power_levels[power_index]
    open_cols = channel_mask.astype(jnp.float32)
    current = solid_temp
    for repeat in range(2):
        padded = jnp.pad(current, ((0, 0), (1, 1), (1, 1)))
        current = advance(padded, conductance, heating, coolant, open_cols)
    paired = current.reshape(coolant.shape[0], 2, current.shape[1], current.shape[2])
    absorbed = 0.08 * open_cols[:, None, :] * (paired[:, 0] + paired[:, 1] - 2.0 * coolant)
    upstream = jnp.cumsum(absorbed, axis=1) - 0.5 * absorbed
    fluid_new = inlet[:, None, :] + flow_gain[:, None, :] * upstream / NX
    return current, fluid_new
```

```python
import functools

import jax
import jax.numpy as jnp
from jax import lax
from jax.experimental import pallas as pl
from jax.experimental.pallas import tpu as pltpu
from jax.sharding import PartitionSpec as P

MESH = pl.DeviceIdType.MESH
LANES = 128
CHUNK = 16


def stencil(src, layer, start, size):
    width = src.shape[2]
    block = src[layer, pl.ds(start, size + 16), :]
    center = block[8 : size + 8]
    above = pltpu.roll(block, 1, 0)[8 : size + 8]
    below = pltpu.roll(block, size + 15, 0)[8 : size + 8]
    lane = lax.broadcasted_iota(jnp.int32, (size, LANES), 1)
    tiles = [center[:, j : j + LANES] for j in range(0, width, LANES)]
    none = jnp.zeros((size, LANES), jnp.float32)
    right_by_one = [none] + [pltpu.roll(t, 1, 1) for t in tiles]
    left_by_one = [pltpu.roll(t, LANES - 1, 1) for t in tiles] + [none]
    sides = []
    for j in range(len(tiles)):
        left = jnp.where(lane == 0, right_by_one[j], right_by_one[j + 1])
        right = jnp.where(lane == LANES - 1, left_by_one[j + 1], left_by_one[j])
        sides.append(left + right)
    return center, above + below + jnp.concatenate(sides, axis=1)


def advance(src, cond, cool, film, heat, start, size, store):
    layers = src.shape[0]
    parts = [stencil(src, l, start, size) for l in range(layers)]
    rows = pl.ds(start, size)
    for l in range(layers):
        k = l // 2
        u, lateral = parts[l]
        near = [parts[m][0] for m in (l - 1, l + 1) if 0 <= m < layers]
        keep = (1.0 - 0.05 * len(near)) - film[k : k + 1, :]
        new = u * keep + cond[l, rows, :] * (lateral - 4.0 * u)
        new = new + 0.05 * (near[0] + near[1] if len(near) == 2 else near[0])
        new = new + film[k : k + 1, :] * cool[k, rows, :]
        if l == 0:
            new = new + heat
        store(l, new)


def pick(index, levels, count):
    values = [levels[i] for i in range(count)]
    bit = 1
    while len(values) > 1:
        if len(values) % 2:
            values.append(values[-1])
        odd = (index & bit) != 0
        values = [jnp.where(odd, values[i + 1], values[i]) for i in range(0, len(values), 2)]
        bit *= 2
    return values[0]


def kernel(
    n_flow, n_cross,
    u_hbm, c_hbm, cool_hbm, idx_hbm, lev_hbm, mask_hbm, inlet_hbm, gain_hbm,
    out, fluid,
    u0, u1, cond, cool, idx, heat, abs_hi, abs_lo, lev, mask, inlet, gain,
    row_out, col_out, row_in, col_in, tot_out, tot_in,
    big_sem, small_sem, halo_send, halo_recv, tot_send, tot_recv,
):
    layers, rows, width = u_hbm.shape
    chans = cool_hbm.shape[0]
    blocks = rows // 8
    per = LANES // layers
    groups = 4 if rows % (4 * CHUNK) == 0 else 1
    span = rows // groups
    me_f, me_c = lax.axis_index("flow"), lax.axis_index("cross")

    def loads(g):
        part = pl.ds(g * span, span)
        return [
            pltpu.make_async_copy(c_hbm.at[:, part], cond.at[:, part], big_sem.at[g, 1]),
            pltpu.make_async_copy(cool_hbm.at[:, part], cool.at[:, part], big_sem.at[g, 2]),
            pltpu.make_async_copy(idx_hbm.at[part], idx.at[part], big_sem.at[g, 3]),
        ]

    def load_u(g):
        return pltpu.make_async_copy(
            u_hbm.at[:, pl.ds(g * span, span)],
            u0.at[:, pl.ds(8 + g * span, span)],
            big_sem.at[g, 0],
        )

    small = [
        pltpu.make_async_copy(src, dst, small_sem.at[i])
        for i, (src, dst) in enumerate(
            [(lev_hbm, lev), (mask_hbm, mask), (inlet_hbm, inlet), (gain_hbm, gain)]
        )
    ]
    for g in range(groups):
        load_u(g).start()
    for s in small:
        s.start()
    for g in range(groups):
        for one in loads(g):
            one.start()

    barrier = pltpu.get_barrier_semaphore()
    for d in range(1, n_flow):
        pl.semaphore_signal(
            barrier, inc=1, device_id=(lax.rem(me_f + d, n_flow), me_c), device_id_type=MESH
        )

    @pl.when(me_c > 0)
    def _():
        pl.semaphore_signal(barrier, inc=1, device_id=(me_f, me_c - 1), device_id_type=MESH)

    @pl.when(me_c < n_cross - 1)
    def _():
        pl.semaphore_signal(barrier, inc=1, device_id=(me_f, me_c + 1), device_id_type=MESH)

    zeros = jnp.zeros((layers, 8, width), jnp.float32)
    for ref in (u0, u1):
        ref[:, 0:8, :] = zeros
        ref[:, rows + 8 : rows + 16, :] = zeros
    col_out[...] = jnp.zeros_like(col_out)
    tot_out[...] = jnp.zeros_like(tot_out)

    has = [me_f > 0, me_f < n_flow - 1, me_c > 0, me_c < n_cross - 1]
    peer = [
        (jnp.maximum(me_f - 1, 0), me_c),
        (jnp.minimum(me_f + 1, n_flow - 1), me_c),
        (me_f, jnp.maximum(me_c - 1, 0)),
        (me_f, jnp.minimum(me_c + 1, n_cross - 1)),
    ]

    def halo(turn, d):
        send, recv = (row_out, row_in) if d < 2 else (col_out, col_in)
        return pltpu.make_async_remote_copy(
            src_ref=send.at[turn, d % 2],
            dst_ref=recv.at[turn, 1 - d % 2],
            send_sem=halo_send.at[turn, d],
            recv_sem=halo_recv.at[turn, d + 1 - 2 * (d % 2)],
            device_id=peer[d],
            device_id_type=MESH,
        )

    def arrival(turn, d):
        recv = row_in if d < 2 else col_in
        return pltpu.make_async_remote_copy(
            src_ref=recv.at[turn, d % 2],
            dst_ref=recv.at[turn, d % 2],
            send_sem=halo_send.at[turn, d],
            recv_sem=halo_recv.at[turn, d],
            device_id=peer[d],
            device_id_type=MESH,
        )

    def send_halos(turn):
        for d in (2, 3, 0, 1):
            @pl.when(has[d])
            def _():
                halo(turn, d).start()

    def take_halos(turn):
        for d in range(4):
            @pl.when(has[d])
            def _():
                arrival(turn, d).wait_recv()

            @pl.when(jnp.logical_not(has[d]))
            def _():
                recv = row_in if d < 2 else col_in
                recv[turn, d % 2] = jnp.zeros(recv.shape[2:], jnp.float32)

    lane = lax.broadcasted_iota(jnp.int32, (8, LANES), 1)

    def pack_cols(turn, b, lefts, rights):
        base = lax.rem(b, per) * layers
        where = pl.ds(pl.multiple_of((b // per) * 8, 8), 8)
        for side, tiles in enumerate((lefts, rights)):
            joined = jnp.zeros((8, LANES), jnp.float32)
            for l, tile in enumerate(tiles):
                shift = (l + side) % LANES
                moved = pltpu.roll(tile, shift, 1) if shift else tile
                joined = jnp.where(lane == l, moved, joined)
            joined = pltpu.roll(joined, base, 1)
            mine = (lane >= base) & (lane < base + layers)
            col_out[turn, side, where, :] = jnp.where(mine, joined, col_out[turn, side, where, :])

    def fix_cols(turn, b, ref, pad):
        base = lax.rem(b, per) * layers
        where = pl.ds(pl.multiple_of((b // per) * 8, 8), 8)
        at = pl.multiple_of(b * 8, 8)
        edges = []
        for side in range(2):
            cols = pl.ds(0, LANES) if side == 0 else pl.ds(width - LANES, LANES)
            target = 0 if side == 0 else LANES - 1
            packed = pltpu.roll(col_in[turn, side, where, :], lax.rem(LANES - base, LANES), 1)
            tiles = []
            for l in range(layers):
                shift = (target - l) % LANES
                beyond = pltpu.roll(packed, shift, 1) if shift else packed
                term = jnp.where(lane == target, beyond * cond[l, pl.ds(at, 8), cols], 0.0)
                tile = ref[l, pl.ds(at + pad, 8), cols] + term
                ref[l, pl.ds(at + pad, 8), cols] = tile
                tiles.append(tile)
            edges.append(tiles)
        return edges

    def fix_rows(turn, ref, pad):
        for l in range(layers):
            for side, row in ((0, 0), (1, rows - 1)):
                at = pl.ds(pad + row, 1)
                ref[l, at, :] = (
                    ref[l, at, :] + cond[l, pl.ds(row, 1), :] * row_in[turn, side, pl.ds(l, 1), :]
                )

    def pack_rows(turn, ref):
        for l in range(layers):
            row_out[turn, 0, pl.ds(l, 1), :] = ref[l, pl.ds(8, 1), :]
            row_out[turn, 1, pl.ds(l, 1), :] = ref[l, pl.ds(rows + 7, 1), :]

    per_group = blocks // groups
    for g in range(groups):
        load_u(g).wait()

        def pack(i, _):
            b = g * per_group + i
            at = pl.ds(pl.multiple_of(b * 8 + 8, 8), 8)
            pack_cols(
                0, b,
                [u0[l, at, pl.ds(0, LANES)] for l in range(layers)],
                [u0[l, at, pl.ds(width - LANES, LANES)] for l in range(layers)],
            )
            return 0

        lax.fori_loop(0, per_group, pack, 0)
    pack_rows(0, u0)
    pl.semaphore_wait(barrier, n_flow - 1 + has[2].astype(jnp.int32) + has[3].astype(jnp.int32))
    send_halos(0)

    for s in small:
        s.wait()
    film = 0.08 * mask[...].astype(jnp.float32)

    for g in range(groups):
        for one in loads(g):
            one.wait()

        def first(i, _):
            start = pl.multiple_of(g * span + i * CHUNK, CHUNK)
            warm = pick(idx[pl.ds(start, CHUNK), :], lev, lev.shape[0])
            heat[pl.ds(start, CHUNK), :] = warm

            def store(l, new):
                u1[l, pl.ds(start + 8, CHUNK), :] = new

            advance(u0, cond, cool, film, warm, start, CHUNK, store)
            return 0

        lax.fori_loop(0, span // CHUNK, first, 0)

    take_halos(0)
    fix_rows(0, u1, 8)

    def fix_first(b, _):
        lefts, rights = fix_cols(0, b, u1, 8)
        pack_cols(1, b, lefts, rights)
        return 0

    lax.fori_loop(0, blocks, fix_first, 0)
    pack_rows(1, u1)
    send_halos(1)

    def second(i, _):
        start = pl.multiple_of(i * CHUNK, CHUNK)

        def store(l, new):
            out[l, pl.ds(start, CHUNK), :] = new

        advance(u1, cond, cool, film, heat[pl.ds(start, CHUNK), :], start, CHUNK, store)
        return 0

    lax.fori_loop(0, rows // CHUNK, second, 0)
    take_halos(1)
    fix_rows(1, out, 0)

    def fix_second(b, _):
        fix_cols(1, b, out, 0)
        return 0

    lax.fori_loop(0, blocks, fix_second, 0)

    def take_up(i, sums):
        at = pl.ds(pl.multiple_of(i * CHUNK, CHUNK), CHUNK)
        new = []
        for k in range(chans):
            taken = film[k : k + 1, :] * (
                out[2 * k, at, :] + out[2 * k + 1, at, :] - 2.0 * cool[k, at, :]
            )
            high = taken.astype(jnp.bfloat16)
            abs_hi[k, at, :] = high
            abs_lo[k, at, :] = (taken - high.astype(jnp.float32)).astype(jnp.bfloat16)
            total = sums[k]
            for s in range(0, CHUNK, 8):
                total = total + taken[s : s + 8]
            new.append(total)
        return tuple(new)

    sums = lax.fori_loop(
        0, rows // CHUNK, take_up,
        tuple(jnp.zeros((8, width), jnp.float32) for _ in range(chans)),
    )
    for k in range(chans):
        tot_out[pl.ds(k, 1), :] = jnp.sum(sums[k], axis=0, keepdims=True)

    def carry(d):
        return pltpu.make_async_remote_copy(
            src_ref=tot_out,
            dst_ref=tot_in.at[d - 1],
            send_sem=tot_send.at[d - 1],
            recv_sem=tot_recv.at[d - 1],
            device_id=(lax.rem(me_f + d, n_flow), me_c),
            device_id_type=MESH,
        )

    for d in range(1, n_flow):
        @pl.when(me_f + d < n_flow)
        def _():
            carry(d).start()

    i_pos = lax.broadcasted_iota(jnp.int32, (rows, rows), 0)
    j_pos = lax.broadcasted_iota(jnp.int32, (rows, rows), 1)
    triangle = jnp.where(j_pos < i_pos, 1.0, jnp.where(j_pos == i_pos, 0.5, 0.0)).astype(
        jnp.bfloat16
    )
    for k in range(chans):
        fluid[k] = jnp.dot(
            triangle, abs_hi[k], preferred_element_type=jnp.float32
        ) + jnp.dot(triangle, abs_lo[k], preferred_element_type=jnp.float32)

    for d in range(1, n_flow):
        @pl.when(me_f >= d)
        def _():
            carry(d).wait_recv()

        @pl.when(me_f < d)
        def _():
            tot_in[d - 1] = jnp.zeros(tot_in.shape[1:], jnp.float32)

    carried = tot_in[0]
    for d in range(2, n_flow):
        carried = carried + tot_in[d - 1]
    scale = gain[...] * (1.0 / (rows * n_flow))
    origin = inlet[...] + scale * carried[:chans]

    def march(i, _):
        at = pl.ds(pl.multiple_of(i * CHUNK, CHUNK), CHUNK)
        for k in range(chans):
            fluid[k, at, :] = origin[k : k + 1, :] + scale[k : k + 1, :] * fluid[k, at, :]
        return 0

    lax.fori_loop(0, rows // CHUNK, march, 0)

    for turn in range(2):
        for d in range(4):
            @pl.when(has[d])
            def _():
                halo(turn, d).wait_send()
    for d in range(1, n_flow):
        @pl.when(me_f + d < n_flow)
        def _():
            carry(d).wait_send()


def shards(
    solid_temp, conductance, coolant, power_index, power_levels, channel_mask, inlet, flow_gain
):
    n_flow, n_cross = lax.axis_size("flow"), lax.axis_size("cross")
    layers, rows, width = solid_temp.shape
    chans = coolant.shape[0]
    f32 = jnp.float32
    packed = pl.cdiv(rows // 8, LANES // layers) * 8
    totals = pl.cdiv(chans, 8) * 8
    scratch = [
        pltpu.VMEM((layers, rows + 16, width), f32),
        pltpu.VMEM((layers, rows + 16, width), f32),
        pltpu.VMEM((layers, rows, width), f32),
        pltpu.VMEM((chans, rows, width), f32),
        pltpu.VMEM((rows, width), jnp.int32),
        pltpu.VMEM((rows, width), f32),
        pltpu.VMEM((chans, rows, width), jnp.bfloat16),
        pltpu.VMEM((chans, rows, width), jnp.bfloat16),
        pltpu.SMEM(power_levels.shape, f32),
        pltpu.VMEM((chans, width), jnp.int32),
        pltpu.VMEM((chans, width), f32),
        pltpu.VMEM((chans, width), f32),
        pltpu.VMEM((2, 2, layers, width), f32),
        pltpu.VMEM((2, 2, packed, LANES), f32),
        pltpu.VMEM((2, 2, layers, width), f32),
        pltpu.VMEM((2, 2, packed, LANES), f32),
        pltpu.VMEM((totals, width), f32),
        pltpu.VMEM((n_flow - 1, totals, width), f32),
        pltpu.SemaphoreType.DMA((4, 4)),
        pltpu.SemaphoreType.DMA((4,)),
        pltpu.SemaphoreType.DMA((2, 4)),
        pltpu.SemaphoreType.DMA((2, 4)),
        pltpu.SemaphoreType.DMA((n_flow - 1,)),
        pltpu.SemaphoreType.DMA((n_flow - 1,)),
    ]
    cells = layers * rows * width
    return pl.pallas_call(
        functools.partial(kernel, n_flow, n_cross),
        out_shape=(
            pltpu.VMEM((layers, rows, width), f32),
            pltpu.VMEM((chans, rows, width), f32),
        ),
        in_specs=[pl.BlockSpec(memory_space=pltpu.HBM)] * 8,
        out_specs=(
            pl.BlockSpec(memory_space=pltpu.VMEM),
            pl.BlockSpec(memory_space=pltpu.VMEM),
        ),
        scratch_shapes=scratch,
        compiler_params=pltpu.CompilerParams(
            collective_id=0, has_side_effects=True, vmem_limit_bytes=57 * 1024 * 1024
        ),
        cost_estimate=pl.CostEstimate(
            flops=40 * cells, bytes_accessed=17 * cells, transcendentals=0
        ),
    )(
        solid_temp, conductance, coolant, power_index, power_levels, channel_mask, inlet, flow_gain
    )


def solution(mesh):
    return jax.shard_map(
        shards,
        mesh=mesh,
        in_specs=(
            P(None, "flow", "cross"),
            P(None, "flow", "cross"),
            P(None, "flow", "cross"),
            P("flow", "cross"),
            P(),
            P(None, "cross"),
            P(None, "cross"),
            P(None, "cross"),
        ),
        out_specs=(P(None, "flow", "cross"), P(None, "flow", "cross")),
        check_vma=False,
    )
```

```python
import functools

import jax
import jax.numpy as jnp
from jax import lax
from jax.experimental import pallas as pl
from jax.experimental.pallas import tpu as pltpu
from jax.sharding import PartitionSpec as P

MESH = pl.DeviceIdType.MESH
LANES = 128
CHUNK = 16
STEP = 32


def stencil(src, layer, start, size):
    width = src.shape[2]
    block = src[layer, pl.ds(start, size + 16), :]
    center = block[8 : size + 8]
    above = pltpu.roll(block, 1, 0)[8 : size + 8]
    below = pltpu.roll(block, size + 15, 0)[8 : size + 8]
    lane = lax.broadcasted_iota(jnp.int32, (size, LANES), 1)
    tiles = [center[:, j : j + LANES] for j in range(0, width, LANES)]
    none = jnp.zeros((size, LANES), jnp.float32)
    right_by_one = [none] + [pltpu.roll(t, 1, 1) for t in tiles]
    left_by_one = [pltpu.roll(t, LANES - 1, 1) for t in tiles] + [none]
    sides = []
    for j in range(len(tiles)):
        left = jnp.where(lane == 0, right_by_one[j], right_by_one[j + 1])
        right = jnp.where(lane == LANES - 1, left_by_one[j + 1], left_by_one[j])
        sides.append(left + right)
    return center, above + below + jnp.concatenate(sides, axis=1)


def advance(src, cond, cool, film, heat, start, size, store):
    layers = src.shape[0]
    parts = [stencil(src, l, start, size) for l in range(layers)]
    rows = pl.ds(start, size)
    for l in range(layers):
        k = l // 2
        u, lateral = parts[l]
        near = [parts[m][0] for m in (l - 1, l + 1) if 0 <= m < layers]
        keep = (1.0 - 0.05 * len(near)) - film[k : k + 1, :]
        new = u * keep + cond[l, rows, :] * (lateral - 4.0 * u)
        new = new + 0.05 * (near[0] + near[1] if len(near) == 2 else near[0])
        new = new + film[k : k + 1, :] * cool[k, rows, :]
        if l == 0:
            new = new + heat
        store(l, new)


def pick(index, levels, count):
    values = [levels[i] for i in range(count)]
    bit = 1
    while len(values) > 1:
        if len(values) % 2:
            values.append(values[-1])
        odd = (index & bit) != 0
        values = [jnp.where(odd, values[i + 1], values[i]) for i in range(0, len(values), 2)]
        bit *= 2
    return values[0]


def kernel(
    n_flow, n_cross,
    u_hbm, c_hbm, cool_hbm, idx_hbm, lev_hbm, mask_hbm, inlet_hbm, gain_hbm,
    out, fluid, ends,
    u0, u1, cond, cool, idx, heat, abs_hi, abs_lo, lev, mask, inlet, gain,
    row_out, col_out, row_in, col_in, tot_out, tot_in,
    big_sem, small_sem, halo_send, halo_recv, tot_send, tot_recv,
):
    layers, rows, width = u_hbm.shape
    chans = cool_hbm.shape[0]
    blocks = rows // 8
    per = LANES // layers
    groups = 4 if rows % (4 * STEP) == 0 else 1
    span = rows // groups
    me_f, me_c = lax.axis_index("flow"), lax.axis_index("cross")

    def loads(g):
        part = pl.ds(g * span, span)
        return [
            pltpu.make_async_copy(c_hbm.at[:, part], cond.at[:, part], big_sem.at[g, 1]),
            pltpu.make_async_copy(cool_hbm.at[:, part], cool.at[:, part], big_sem.at[g, 2]),
            pltpu.make_async_copy(idx_hbm.at[part], idx.at[part], big_sem.at[g, 3]),
        ]

    def load_u(g):
        return pltpu.make_async_copy(
            u_hbm.at[:, pl.ds(g * span, span)],
            u0.at[:, pl.ds(8 + g * span, span)],
            big_sem.at[g, 0],
        )

    small = [
        pltpu.make_async_copy(src, dst, small_sem.at[i])
        for i, (src, dst) in enumerate(
            [(lev_hbm, lev), (mask_hbm, mask), (inlet_hbm, inlet), (gain_hbm, gain)]
        )
    ]
    for g in range(groups):
        load_u(g).start()
    for s in small:
        s.start()
    for g in range(groups):
        for one in loads(g):
            one.start()

    barrier = pltpu.get_barrier_semaphore()
    for d in range(1, n_flow):
        pl.semaphore_signal(
            barrier, inc=1, device_id=(lax.rem(me_f + d, n_flow), me_c), device_id_type=MESH
        )

    @pl.when(me_c > 0)
    def _():
        pl.semaphore_signal(barrier, inc=1, device_id=(me_f, me_c - 1), device_id_type=MESH)

    @pl.when(me_c < n_cross - 1)
    def _():
        pl.semaphore_signal(barrier, inc=1, device_id=(me_f, me_c + 1), device_id_type=MESH)

    zeros = jnp.zeros((layers, 8, width), jnp.float32)
    for ref in (u0, u1):
        ref[:, 0:8, :] = zeros
        ref[:, rows + 8 : rows + 16, :] = zeros
    col_out[...] = jnp.zeros_like(col_out)
    tot_out[...] = jnp.zeros_like(tot_out)

    has = [me_f > 0, me_f < n_flow - 1, me_c > 0, me_c < n_cross - 1]
    peer = [
        (jnp.maximum(me_f - 1, 0), me_c),
        (jnp.minimum(me_f + 1, n_flow - 1), me_c),
        (me_f, jnp.maximum(me_c - 1, 0)),
        (me_f, jnp.minimum(me_c + 1, n_cross - 1)),
    ]

    def halo(turn, d):
        send, recv = (row_out, row_in) if d < 2 else (col_out, col_in)
        return pltpu.make_async_remote_copy(
            src_ref=send.at[turn, d % 2],
            dst_ref=recv.at[turn, 1 - d % 2],
            send_sem=halo_send.at[turn, d],
            recv_sem=halo_recv.at[turn, d + 1 - 2 * (d % 2)],
            device_id=peer[d],
            device_id_type=MESH,
        )

    def arrival(turn, d):
        recv = row_in if d < 2 else col_in
        return pltpu.make_async_remote_copy(
            src_ref=recv.at[turn, d % 2],
            dst_ref=recv.at[turn, d % 2],
            send_sem=halo_send.at[turn, d],
            recv_sem=halo_recv.at[turn, d],
            device_id=peer[d],
            device_id_type=MESH,
        )

    def send_halos(turn):
        for d in (2, 3, 0, 1):
            @pl.when(has[d])
            def _():
                halo(turn, d).start()

    def take_halos(turn):
        for d in range(4):
            @pl.when(has[d])
            def _():
                arrival(turn, d).wait_recv()

            @pl.when(jnp.logical_not(has[d]))
            def _():
                recv = row_in if d < 2 else col_in
                recv[turn, d % 2] = jnp.zeros(recv.shape[2:], jnp.float32)

    lane = lax.broadcasted_iota(jnp.int32, (8, LANES), 1)
    group = min(per, blocks)
    edge_cols = (pl.ds(0, LANES), pl.ds(width - LANES, LANES))
    is_layer = [lax.rem(lane, layers) == l for l in range(layers)]
    is_block = [lane // layers == i for i in range(group)]

    def turned(tile, shift):
        return pltpu.roll(tile, shift % LANES, 1) if shift % LANES else tile

    def pack_cols(turn, v, side, tile_of):
        packed = jnp.zeros((8, LANES), jnp.float32)
        for i in range(group):
            joined = jnp.zeros((8, LANES), jnp.float32)
            for l in range(layers):
                joined = jnp.where(is_layer[l], turned(tile_of(i, l), i * layers + l + side), joined)
            packed = jnp.where(is_block[i], joined, packed)
        col_out[turn, side, pl.ds(pl.multiple_of(v * 8, 8), 8), :] = packed

    def fix_cols(turn, v, side, ref, pad):
        target = side * (LANES - 1)
        packed = col_in[turn, side, pl.ds(pl.multiple_of(v * 8, 8), 8), :]
        edge = lane == target
        tiles = {}
        for i in range(group):
            at = pl.multiple_of((v * group + i) * 8, 8)
            for l in range(layers):
                beyond = jnp.where(edge, turned(packed, target - i * layers - l), 0.0)
                tile = ref[l, pl.ds(at + pad, 8), edge_cols[side]]
                tile = tile + beyond * cond[l, pl.ds(at, 8), edge_cols[side]]
                ref[l, pl.ds(at + pad, 8), edge_cols[side]] = tile
                tiles[i, l] = tile
        return lambda i, l: tiles[i, l]

    def fix_rows(turn, ref, pad):
        for l in range(layers):
            for side, row in ((0, 0), (1, rows - 1)):
                at = pl.ds(pad + row, 1)
                ref[l, at, :] = (
                    ref[l, at, :] + cond[l, pl.ds(row, 1), :] * row_in[turn, side, pl.ds(l, 1), :]
                )

    def pack_rows(turn, ref):
        for l in range(layers):
            row_out[turn, 0, pl.ds(l, 1), :] = ref[l, pl.ds(8, 1), :]
            row_out[turn, 1, pl.ds(l, 1), :] = ref[l, pl.ds(rows + 7, 1), :]

    for g in range(groups):
        load_u(g).wait()

    def pack_first(v, _):
        for side in range(2):
            pack_cols(
                0, v, side,
                lambda i, l: u0[
                    l,
                    pl.ds(pl.multiple_of((v * group + i) * 8 + 8, 8), 8),
                    edge_cols[side],
                ],
            )
        return 0

    lax.fori_loop(0, blocks // group, pack_first, 0)
    pack_rows(0, u0)
    pl.semaphore_wait(barrier, n_flow - 1 + has[2].astype(jnp.int32) + has[3].astype(jnp.int32))
    send_halos(0)

    for s in small:
        s.wait()
    film = 0.08 * mask[...].astype(jnp.float32)

    for g in range(groups):
        for one in loads(g):
            one.wait()

        def first(i, _):
            start = pl.multiple_of(g * span + i * STEP, STEP)
            warm = pick(idx[pl.ds(start, STEP), :], lev, lev.shape[0])
            heat[pl.ds(start, STEP), :] = warm

            def store(l, new):
                u1[l, pl.ds(start + 8, STEP), :] = new

            advance(u0, cond, cool, film, warm, start, STEP, store)
            return 0

        lax.fori_loop(0, span // STEP, first, 0)

    take_halos(0)
    fix_rows(0, u1, 8)

    def fix_first(v, _):
        for side in range(2):
            pack_cols(1, v, side, fix_cols(0, v, side, u1, 8))
        return 0

    lax.fori_loop(0, blocks // group, fix_first, 0)
    pack_rows(1, u1)
    send_halos(1)

    def second(i, _):
        start = pl.multiple_of(i * STEP, STEP)

        def store(l, new):
            out[l, pl.ds(start, STEP), :] = new

        advance(u1, cond, cool, film, heat[pl.ds(start, STEP), :], start, STEP, store)
        return 0

    lax.fori_loop(0, rows // STEP, second, 0)
    take_halos(1)
    fix_rows(1, out, 0)

    def fix_second(v, _):
        for side in range(2):
            fix_cols(1, v, side, out, 0)
        return 0

    lax.fori_loop(0, blocks // group, fix_second, 0)

    def take_up(i, sums):
        at = pl.ds(pl.multiple_of(i * CHUNK, CHUNK), CHUNK)
        new = []
        for k in range(chans):
            taken = film[k : k + 1, :] * (
                out[2 * k, at, :] + out[2 * k + 1, at, :] - 2.0 * cool[k, at, :]
            )
            high = taken.astype(jnp.bfloat16)
            abs_hi[k, at, :] = high
            abs_lo[k, at, :] = (taken - high.astype(jnp.float32)).astype(jnp.bfloat16)
            total = sums[k]
            for s in range(0, CHUNK, 8):
                total = total + taken[s : s + 8]
            new.append(total)
        return tuple(new)

    sums = lax.fori_loop(
        0, rows // CHUNK, take_up,
        tuple(jnp.zeros((8, width), jnp.float32) for _ in range(chans)),
    )
    for k in range(chans):
        tot_out[pl.ds(k, 1), :] = jnp.sum(sums[k], axis=0, keepdims=True)

    def carry(d):
        return pltpu.make_async_remote_copy(
            src_ref=tot_out,
            dst_ref=tot_in.at[d - 1],
            send_sem=tot_send.at[d - 1],
            recv_sem=tot_recv.at[d - 1],
            device_id=(lax.rem(me_f + d, n_flow), me_c),
            device_id_type=MESH,
        )

    for d in range(1, n_flow):
        @pl.when(me_f + d < n_flow)
        def _():
            carry(d).start()

    i_pos = lax.broadcasted_iota(jnp.int32, (rows, rows), 0)
    j_pos = lax.broadcasted_iota(jnp.int32, (rows, rows), 1)
    triangle = jnp.where(j_pos < i_pos, 1.0, jnp.where(j_pos == i_pos, 0.5, 0.0)).astype(
        jnp.bfloat16
    )
    for k in range(chans):
        fluid[k] = jnp.dot(
            triangle, abs_hi[k], preferred_element_type=jnp.float32
        ) + jnp.dot(triangle, abs_lo[k], preferred_element_type=jnp.float32)

    for d in range(1, n_flow):
        @pl.when(me_f >= d)
        def _():
            carry(d).wait_recv()

        @pl.when(me_f < d)
        def _():
            tot_in[d - 1] = jnp.zeros(tot_in.shape[1:], jnp.float32)

    carried = tot_in[0]
    for d in range(2, n_flow):
        carried = carried + tot_in[d - 1]
    scale = gain[...] * (1.0 / (rows * n_flow))
    ends[0] = inlet[...] + scale * carried[:chans]
    ends[1] = scale

    for turn in range(2):
        for d in range(4):
            @pl.when(has[d])
            def _():
                halo(turn, d).wait_send()
    for d in range(1, n_flow):
        @pl.when(me_f + d < n_flow)
        def _():
            carry(d).wait_send()


def finish(solid, within, ends, out, fluid, held, solid_sem, fluid_sem):
    chans, rows, _ = within.shape
    whole = pltpu.make_async_copy(solid, out, solid_sem)
    whole.start()
    parts = []
    for k in range(chans):
        def march(i, _):
            at = pl.ds(pl.multiple_of(i * STEP, STEP), STEP)
            held[k, at, :] = ends[0, k : k + 1, :] + ends[1, k : k + 1, :] * within[k, at, :]
            return 0

        lax.fori_loop(0, rows // STEP, march, 0)
        parts.append(pltpu.make_async_copy(held.at[k], fluid.at[k], fluid_sem.at[k]))
        parts[k].start()
    whole.wait()
    for part in parts:
        part.wait()


def shards(
    solid_temp, conductance, coolant, power_index, power_levels, channel_mask, inlet, flow_gain
):
    n_flow, n_cross = lax.axis_size("flow"), lax.axis_size("cross")
    layers, rows, width = solid_temp.shape
    chans = coolant.shape[0]
    f32 = jnp.float32
    packed = pl.cdiv(rows // 8, LANES // layers) * 8
    totals = pl.cdiv(chans, 8) * 8
    scratch = [
        pltpu.VMEM((layers, rows + 16, width), f32),
        pltpu.VMEM((layers, rows + 16, width), f32),
        pltpu.VMEM((layers, rows, width), f32),
        pltpu.VMEM((chans, rows, width), f32),
        pltpu.VMEM((rows, width), jnp.int32),
        pltpu.VMEM((rows, width), f32),
        pltpu.VMEM((chans, rows, width), jnp.bfloat16),
        pltpu.VMEM((chans, rows, width), jnp.bfloat16),
        pltpu.SMEM(power_levels.shape, f32),
        pltpu.VMEM((chans, width), jnp.int32),
        pltpu.VMEM((chans, width), f32),
        pltpu.VMEM((chans, width), f32),
        pltpu.VMEM((2, 2, layers, width), f32),
        pltpu.VMEM((2, 2, packed, LANES), f32),
        pltpu.VMEM((2, 2, layers, width), f32),
        pltpu.VMEM((2, 2, packed, LANES), f32),
        pltpu.VMEM((totals, width), f32),
        pltpu.VMEM((n_flow - 1, totals, width), f32),
        pltpu.SemaphoreType.DMA((4, 4)),
        pltpu.SemaphoreType.DMA((4,)),
        pltpu.SemaphoreType.DMA((2, 4)),
        pltpu.SemaphoreType.DMA((2, 4)),
        pltpu.SemaphoreType.DMA((n_flow - 1,)),
        pltpu.SemaphoreType.DMA((n_flow - 1,)),
    ]
    cells = layers * rows * width
    limit = 57 * 1024 * 1024
    solid, within, ends = pl.pallas_call(
        functools.partial(kernel, n_flow, n_cross),
        out_shape=(
            pltpu.VMEM((layers, rows, width), f32),
            pltpu.VMEM((chans, rows, width), f32),
            pltpu.VMEM((2, chans, width), f32),
        ),
        in_specs=[pl.BlockSpec(memory_space=pltpu.HBM)] * 8,
        out_specs=(pl.BlockSpec(memory_space=pltpu.VMEM),) * 3,
        scratch_shapes=scratch,
        compiler_params=pltpu.CompilerParams(
            collective_id=0, has_side_effects=True, vmem_limit_bytes=limit
        ),
        cost_estimate=pl.CostEstimate(
            flops=40 * cells, bytes_accessed=11 * cells, transcendentals=0
        ),
    )(
        solid_temp, conductance, coolant, power_index, power_levels, channel_mask, inlet, flow_gain
    )
    return pl.pallas_call(
        finish,
        out_shape=(
            jax.ShapeDtypeStruct((layers, rows, width), f32),
            jax.ShapeDtypeStruct((chans, rows, width), f32),
        ),
        in_specs=[pl.BlockSpec(memory_space=pltpu.VMEM)] * 3,
        out_specs=(pl.BlockSpec(memory_space=pltpu.HBM),) * 2,
        scratch_shapes=[
            pltpu.VMEM((chans, rows, width), f32),
            pltpu.SemaphoreType.DMA,
            pltpu.SemaphoreType.DMA((chans,)),
        ],
        compiler_params=pltpu.CompilerParams(vmem_limit_bytes=16 * 1024 * 1024),
        cost_estimate=pl.CostEstimate(flops=cells, bytes_accessed=6 * cells, transcendentals=0),
    )(solid, within, ends)


def solution(mesh):
    return jax.shard_map(
        shards,
        mesh=mesh,
        in_specs=(
            P(None, "flow", "cross"),
            P(None, "flow", "cross"),
            P(None, "flow", "cross"),
            P("flow", "cross"),
            P(),
            P(None, "cross"),
            P(None, "cross"),
            P(None, "cross"),
        ),
        out_specs=(P(None, "flow", "cross"), P(None, "flow", "cross")),
        check_vma=False,
    )
```

```python
import functools

import jax
import jax.numpy as jnp
from jax import lax
from jax.experimental import pallas as pl
from jax.experimental.pallas import tpu as pltpu
from jax.sharding import PartitionSpec as P

MESH = pl.DeviceIdType.MESH
LANES = 128
CHUNK = 32
STEP = 32


def stencil(src, layer, start, size):
    count = src.shape[1]
    lane = lax.broadcasted_iota(jnp.int32, (size, LANES), 1)
    tiles = [src[layer, j, pl.ds(start + 8, size), :] for j in range(count)]
    none = jnp.zeros((size, LANES), jnp.float32)
    right_by_one = [none] + [pltpu.roll(t, 1, 1) for t in tiles]
    left_by_one = [pltpu.roll(t, LANES - 1, 1) for t in tiles] + [none]
    sums = []
    for j in range(count):
        left = jnp.where(lane == 0, right_by_one[j], right_by_one[j + 1])
        right = jnp.where(lane == LANES - 1, left_by_one[j + 1], left_by_one[j])
        above = src[layer, j, pl.ds(start + 7, size), :]
        below = src[layer, j, pl.ds(start + 9, size), :]
        sums.append((left + right) + (above + below))
    return jnp.concatenate(tiles, axis=1), jnp.concatenate(sums, axis=1)


def advance(src, cond, cool, film, heat, start, size, store):
    layers = src.shape[0]
    parts = [stencil(src, l, start, size) for l in range(layers)]
    rows = pl.ds(start, size)
    for l in range(layers):
        k = l // 2
        u, lateral = parts[l]
        near = [parts[m][0] for m in (l - 1, l + 1) if 0 <= m < layers]
        keep = (1.0 - 0.05 * len(near)) - film[k : k + 1, :]
        new = u * keep + cond[l, rows, :] * (lateral - 4.0 * u)
        new = new + 0.05 * (near[0] + near[1] if len(near) == 2 else near[0])
        new = new + film[k : k + 1, :] * cool[k, rows, :]
        if l == 0:
            new = new + heat
        store(l, new)


def pick(index, levels, count):
    values = [levels[i] for i in range(count)]
    bit = 1
    while len(values) > 1:
        if len(values) % 2:
            values.append(values[-1])
        odd = (index & bit) != 0
        values = [jnp.where(odd, values[i + 1], values[i]) for i in range(0, len(values), 2)]
        bit *= 2
    return values[0]


def kernel(
    n_flow, n_cross,
    u_hbm, c_hbm, cool_hbm, idx_hbm, lev_hbm, mask_hbm, inlet_hbm, gain_hbm,
    out, fluid, ends,
    u0, u1, cond, cool, idx, heat, lev, mask, inlet, gain,
    row_out, col_out, row_in, col_in, tot_out, tot_in,
    u_sem, big_sem, small_sem, halo_send, halo_recv, tot_send, tot_recv,
):
    layers, rows, width = u_hbm.shape
    chans = cool_hbm.shape[0]
    blocks = rows // 8
    per = LANES // layers
    groups = 4 if rows % (4 * STEP) == 0 else 1
    span = rows // groups
    lane_tiles = width // LANES
    edge_tiles = (0, lane_tiles - 1)
    me_f, me_c = lax.axis_index("flow"), lax.axis_index("cross")

    def loads(g):
        part = pl.ds(g * span, span)
        return [
            pltpu.make_async_copy(c_hbm.at[:, part], cond.at[:, part], big_sem.at[g, 1]),
            pltpu.make_async_copy(cool_hbm.at[:, part], cool.at[:, part], big_sem.at[g, 2]),
            pltpu.make_async_copy(idx_hbm.at[part], idx.at[part], big_sem.at[g, 3]),
        ]

    def load_u(g):
        return [
            pltpu.make_async_copy(
                u_hbm.at[:, pl.ds(g * span, span), pl.ds(j * LANES, LANES)],
                u0.at[:, j, pl.ds(8 + g * span, span)],
                u_sem.at[g, j],
            )
            for j in range(lane_tiles)
        ]

    small = [
        pltpu.make_async_copy(src, dst, small_sem.at[i])
        for i, (src, dst) in enumerate(
            [(lev_hbm, lev), (mask_hbm, mask), (inlet_hbm, inlet), (gain_hbm, gain)]
        )
    ]
    for g in range(groups):
        for one in load_u(g):
            one.start()
    for s in small:
        s.start()
    for g in range(groups):
        for one in loads(g):
            one.start()

    barrier = pltpu.get_barrier_semaphore()
    for d in range(1, n_flow):
        pl.semaphore_signal(
            barrier, inc=1, device_id=(lax.rem(me_f + d, n_flow), me_c), device_id_type=MESH
        )

    @pl.when(me_c > 0)
    def _():
        pl.semaphore_signal(barrier, inc=1, device_id=(me_f, me_c - 1), device_id_type=MESH)

    @pl.when(me_c < n_cross - 1)
    def _():
        pl.semaphore_signal(barrier, inc=1, device_id=(me_f, me_c + 1), device_id_type=MESH)

    zeros = jnp.zeros((layers, lane_tiles, 8, LANES), jnp.float32)
    for ref in (u0, u1):
        ref[:, :, 0:8, :] = zeros
        ref[:, :, rows + 8 : rows + 16, :] = zeros
    col_out[...] = jnp.zeros_like(col_out)
    tot_out[...] = jnp.zeros_like(tot_out)

    has = [me_f > 0, me_f < n_flow - 1, me_c > 0, me_c < n_cross - 1]
    peer = [
        (jnp.maximum(me_f - 1, 0), me_c),
        (jnp.minimum(me_f + 1, n_flow - 1), me_c),
        (me_f, jnp.maximum(me_c - 1, 0)),
        (me_f, jnp.minimum(me_c + 1, n_cross - 1)),
    ]

    def halo(turn, d):
        send, recv = (row_out, row_in) if d < 2 else (col_out, col_in)
        return pltpu.make_async_remote_copy(
            src_ref=send.at[turn, d % 2],
            dst_ref=recv.at[turn, 1 - d % 2],
            send_sem=halo_send.at[turn, d],
            recv_sem=halo_recv.at[turn, d + 1 - 2 * (d % 2)],
            device_id=peer[d],
            device_id_type=MESH,
        )

    def arrival(turn, d):
        recv = row_in if d < 2 else col_in
        return pltpu.make_async_remote_copy(
            src_ref=recv.at[turn, d % 2],
            dst_ref=recv.at[turn, d % 2],
            send_sem=halo_send.at[turn, d],
            recv_sem=halo_recv.at[turn, d],
            device_id=peer[d],
            device_id_type=MESH,
        )

    def send_halos(turn):
        for d in (2, 3, 0, 1):
            @pl.when(has[d])
            def _():
                halo(turn, d).start()

    def take_halos(turn):
        for d in range(4):
            @pl.when(has[d])
            def _():
                arrival(turn, d).wait_recv()

            @pl.when(jnp.logical_not(has[d]))
            def _():
                recv = row_in if d < 2 else col_in
                recv[turn, d % 2] = jnp.zeros(recv.shape[2:], jnp.float32)

    lane = lax.broadcasted_iota(jnp.int32, (8, LANES), 1)
    group = min(per, blocks)
    edge_cols = (pl.ds(0, LANES), pl.ds(width - LANES, LANES))
    is_layer = [lax.rem(lane, layers) == l for l in range(layers)]
    is_block = [lane // layers == i for i in range(group)]

    def turned(tile, shift):
        return pltpu.roll(tile, shift % LANES, 1) if shift % LANES else tile

    def pack_cols(turn, v, side, tile_of):
        packed = jnp.zeros((8, LANES), jnp.float32)
        for i in range(group):
            joined = jnp.zeros((8, LANES), jnp.float32)
            for l in range(layers):
                joined = jnp.where(is_layer[l], turned(tile_of(i, l), i * layers + l + side), joined)
            packed = jnp.where(is_block[i], joined, packed)
        col_out[turn, side, pl.ds(pl.multiple_of(v * 8, 8), 8), :] = packed

    def fix_cols(turn, v, side, view):
        target = side * (LANES - 1)
        packed = col_in[turn, side, pl.ds(pl.multiple_of(v * 8, 8), 8), :]
        edge = lane == target
        tiles = {}
        for i in range(group):
            at = pl.multiple_of((v * group + i) * 8, 8)
            for l in range(layers):
                beyond = jnp.where(edge, turned(packed, target - i * layers - l), 0.0)
                ref, where = view(side, l, at)
                tile = ref[where] + beyond * cond[l, pl.ds(at, 8), edge_cols[side]]
                ref[where] = tile
                tiles[i, l] = tile
        return lambda i, l: tiles[i, l]

    def lane_tile(j):
        return pl.ds(j * LANES, LANES)

    def in_u1(side, l, at):
        return u1, (l, edge_tiles[side], pl.ds(at + 8, 8), slice(None))

    def in_out(side, l, at):
        return out, (l, pl.ds(at, 8), edge_cols[side])

    def beyond_rows(turn, l, side, row, j):
        return (
            cond[l, pl.ds(row, 1), lane_tile(j)] * row_in[turn, side, pl.ds(l, 1), lane_tile(j)]
        )

    def fix_rows(turn, final):
        for l in range(layers):
            for side, row in ((0, 0), (1, rows - 1)):
                for j in range(lane_tiles):
                    term = beyond_rows(turn, l, side, row, j)
                    if final:
                        where = (l, pl.ds(row, 1), lane_tile(j))
                        out[where] = out[where] + term
                    else:
                        where = (l, j, pl.ds(row + 8, 1), slice(None))
                        u1[where] = u1[where] + term

    def pack_rows(turn, ref):
        for l in range(layers):
            for j in range(lane_tiles):
                for side, row in ((0, 8), (1, rows + 7)):
                    row_out[turn, side, pl.ds(l, 1), lane_tile(j)] = ref[l, j, pl.ds(row, 1), :]

    for g in range(groups):
        for one in load_u(g):
            one.wait()

    def pack_first(v, _):
        for side in range(2):
            pack_cols(
                0, v, side,
                lambda i, l: u0[
                    l,
                    edge_tiles[side],
                    pl.ds(pl.multiple_of((v * group + i) * 8 + 8, 8), 8),
                    :,
                ],
            )
        return 0

    lax.fori_loop(0, blocks // group, pack_first, 0)
    pack_rows(0, u0)
    pl.semaphore_wait(barrier, n_flow - 1 + has[2].astype(jnp.int32) + has[3].astype(jnp.int32))
    send_halos(0)

    for s in small:
        s.wait()
    film = 0.08 * mask[...].astype(jnp.float32)

    for g in range(groups):
        for one in loads(g):
            one.wait()

        def first(i, _):
            start = pl.multiple_of(g * span + i * STEP, STEP)
            warm = pick(idx[pl.ds(start, STEP), :], lev, lev.shape[0])
            heat[pl.ds(start, STEP), :] = warm

            def store(l, new):
                for j in range(lane_tiles):
                    u1[l, j, pl.ds(start + 8, STEP), :] = new[:, j * LANES : (j + 1) * LANES]

            advance(u0, cond, cool, film, warm, start, STEP, store)
            return 0

        lax.fori_loop(0, span // STEP, first, 0)

    take_halos(0)
    fix_rows(0, False)

    def fix_first(v, _):
        for side in range(2):
            pack_cols(1, v, side, fix_cols(0, v, side, in_u1))
        return 0

    lax.fori_loop(0, blocks // group, fix_first, 0)
    pack_rows(1, u1)
    send_halos(1)

    def second(i, _):
        start = pl.multiple_of(i * STEP, STEP)

        def store(l, new):
            out[l, pl.ds(start, STEP), :] = new

        advance(u1, cond, cool, film, heat[pl.ds(start, STEP), :], start, STEP, store)
        return 0

    lax.fori_loop(0, rows // STEP, second, 0)
    take_halos(1)
    fix_rows(1, True)

    def fix_second(v, _):
        for side in range(2):
            fix_cols(1, v, side, in_out)
        return 0

    lax.fori_loop(0, blocks // group, fix_second, 0)

    def take_up(i, sums):
        at = pl.ds(pl.multiple_of(i * CHUNK, CHUNK), CHUNK)
        new = []
        for k in range(chans):
            taken = film[k : k + 1, :] * (
                out[2 * k, at, :] + out[2 * k + 1, at, :] - 2.0 * cool[k, at, :]
            )
            fluid[k, at, :] = taken
            total = sums[k]
            for s in range(0, CHUNK, 8):
                total = total + taken[s : s + 8]
            new.append(total)
        return tuple(new)

    sums = lax.fori_loop(
        0, rows // CHUNK, take_up,
        tuple(jnp.zeros((8, width), jnp.float32) for _ in range(chans)),
    )
    for k in range(chans):
        tot_out[pl.ds(k, 1), :] = jnp.sum(sums[k], axis=0, keepdims=True)

    def carry(d):
        return pltpu.make_async_remote_copy(
            src_ref=tot_out,
            dst_ref=tot_in.at[d - 1],
            send_sem=tot_send.at[d - 1],
            recv_sem=tot_recv.at[d - 1],
            device_id=(lax.rem(me_f + d, n_flow), me_c),
            device_id_type=MESH,
        )

    for d in range(1, n_flow):
        @pl.when(me_f + d < n_flow)
        def _():
            carry(d).start()

    i_pos = lax.broadcasted_iota(jnp.int32, (rows, rows), 0)
    j_pos = lax.broadcasted_iota(jnp.int32, (rows, rows), 1)
    triangle = jnp.where(j_pos < i_pos, 1.0, jnp.where(j_pos == i_pos, 0.5, 0.0)).astype(
        jnp.bfloat16
    )
    part = 2 * LANES if width % (2 * LANES) == 0 else LANES
    for k in range(chans):
        for j in range(0, width, part):
            cols = pl.ds(j, part)
            taken = fluid[k, :, cols]
            high = taken.astype(jnp.bfloat16)
            low = (taken - high.astype(jnp.float32)).astype(jnp.bfloat16)
            fluid[k, :, cols] = jnp.dot(
                triangle, high, preferred_element_type=jnp.float32
            ) + jnp.dot(triangle, low, preferred_element_type=jnp.float32)

    for d in range(1, n_flow):
        @pl.when(me_f >= d)
        def _():
            carry(d).wait_recv()

        @pl.when(me_f < d)
        def _():
            tot_in[d - 1] = jnp.zeros(tot_in.shape[1:], jnp.float32)

    carried = tot_in[0]
    for d in range(2, n_flow):
        carried = carried + tot_in[d - 1]
    scale = gain[...] * (1.0 / (rows * n_flow))
    ends[0] = inlet[...] + scale * carried[:chans]
    ends[1] = scale

    for turn in range(2):
        for d in range(4):
            @pl.when(has[d])
            def _():
                halo(turn, d).wait_send()
    for d in range(1, n_flow):
        @pl.when(me_f + d < n_flow)
        def _():
            carry(d).wait_send()


def finish(solid, within, ends, out, fluid, held, solid_sem, fluid_sem):
    chans, rows, _ = within.shape
    whole = pltpu.make_async_copy(solid, out, solid_sem)
    whole.start()
    parts = []
    for k in range(chans):
        def march(i, _):
            at = pl.ds(pl.multiple_of(i * STEP, STEP), STEP)
            held[k, at, :] = ends[0, k : k + 1, :] + ends[1, k : k + 1, :] * within[k, at, :]
            return 0

        lax.fori_loop(0, rows // STEP, march, 0)
        parts.append(pltpu.make_async_copy(held.at[k], fluid.at[k], fluid_sem.at[k]))
        parts[k].start()
    whole.wait()
    for part in parts:
        part.wait()


def shards(
    solid_temp, conductance, coolant, power_index, power_levels, channel_mask, inlet, flow_gain
):
    n_flow, n_cross = lax.axis_size("flow"), lax.axis_size("cross")
    layers, rows, width = solid_temp.shape
    chans = coolant.shape[0]
    f32 = jnp.float32
    packed = pl.cdiv(rows // 8, LANES // layers) * 8
    totals = pl.cdiv(chans, 8) * 8
    scratch = [
        pltpu.VMEM((layers, width // LANES, rows + 16, LANES), f32),
        pltpu.VMEM((layers, width // LANES, rows + 16, LANES), f32),
        pltpu.VMEM((layers, rows, width), f32),
        pltpu.VMEM((chans, rows, width), f32),
        pltpu.VMEM((rows, width), jnp.int32),
        pltpu.VMEM((rows, width), f32),
        pltpu.SMEM(power_levels.shape, f32),
        pltpu.VMEM((chans, width), jnp.int32),
        pltpu.VMEM((chans, width), f32),
        pltpu.VMEM((chans, width), f32),
        pltpu.VMEM((2, 2, layers, width), f32),
        pltpu.VMEM((2, 2, packed, LANES), f32),
        pltpu.VMEM((2, 2, layers, width), f32),
        pltpu.VMEM((2, 2, packed, LANES), f32),
        pltpu.VMEM((totals, width), f32),
        pltpu.VMEM((n_flow - 1, totals, width), f32),
        pltpu.SemaphoreType.DMA((4, width // LANES)),
        pltpu.SemaphoreType.DMA((4, 4)),
        pltpu.SemaphoreType.DMA((4,)),
        pltpu.SemaphoreType.DMA((2, 4)),
        pltpu.SemaphoreType.DMA((2, 4)),
        pltpu.SemaphoreType.DMA((n_flow - 1,)),
        pltpu.SemaphoreType.DMA((n_flow - 1,)),
    ]
    cells = layers * rows * width
    limit = 57 * 1024 * 1024
    solid, within, ends = pl.pallas_call(
        functools.partial(kernel, n_flow, n_cross),
        out_shape=(
            pltpu.VMEM((layers, rows, width), f32),
            pltpu.VMEM((chans, rows, width), f32),
            pltpu.VMEM((2, chans, width), f32),
        ),
        in_specs=[pl.BlockSpec(memory_space=pltpu.HBM)] * 8,
        out_specs=(pl.BlockSpec(memory_space=pltpu.VMEM),) * 3,
        scratch_shapes=scratch,
        compiler_params=pltpu.CompilerParams(
            collective_id=0, has_side_effects=True, vmem_limit_bytes=limit
        ),
        cost_estimate=pl.CostEstimate(
            flops=40 * cells, bytes_accessed=11 * cells, transcendentals=0
        ),
    )(
        solid_temp, conductance, coolant, power_index, power_levels, channel_mask, inlet, flow_gain
    )
    return pl.pallas_call(
        finish,
        out_shape=(
            jax.ShapeDtypeStruct((layers, rows, width), f32),
            jax.ShapeDtypeStruct((chans, rows, width), f32),
        ),
        in_specs=[pl.BlockSpec(memory_space=pltpu.VMEM)] * 3,
        out_specs=(pl.BlockSpec(memory_space=pltpu.HBM),) * 2,
        scratch_shapes=[
            pltpu.VMEM((chans, rows, width), f32),
            pltpu.SemaphoreType.DMA,
            pltpu.SemaphoreType.DMA((chans,)),
        ],
        compiler_params=pltpu.CompilerParams(vmem_limit_bytes=16 * 1024 * 1024),
        cost_estimate=pl.CostEstimate(flops=cells, bytes_accessed=6 * cells, transcendentals=0),
    )(solid, within, ends)


def solution(mesh):
    return jax.shard_map(
        shards,
        mesh=mesh,
        in_specs=(
            P(None, "flow", "cross"),
            P(None, "flow", "cross"),
            P(None, "flow", "cross"),
            P("flow", "cross"),
            P(),
            P(None, "cross"),
            P(None, "cross"),
            P(None, "cross"),
        ),
        out_specs=(P(None, "flow", "cross"), P(None, "flow", "cross")),
        check_vma=False,
    )
```

```python
import functools

import jax
import jax.numpy as jnp
from jax import lax
from jax.experimental import pallas as pl
from jax.experimental.pallas import tpu as pltpu
from jax.sharding import PartitionSpec as P

MESH = pl.DeviceIdType.MESH
LANES = 128
CHUNK = 32
STEP = 32


def lateral_sum(src, layer, tiles, start, size):
    count = len(tiles)
    lane = lax.broadcasted_iota(jnp.int32, (size, LANES), 1)
    none = jnp.zeros((size, LANES), jnp.float32)
    right_by_one = [none] + [pltpu.roll(t, 1, 1) for t in tiles]
    left_by_one = [pltpu.roll(t, LANES - 1, 1) for t in tiles] + [none]
    sums = []
    for j in range(count):
        left = jnp.where(lane == 0, right_by_one[j], right_by_one[j + 1])
        right = jnp.where(lane == LANES - 1, left_by_one[j + 1], left_by_one[j])
        above = src[layer, j, pl.ds(start + 7, size), :]
        below = src[layer, j, pl.ds(start + 9, size), :]
        sums.append((left + right) + (above + below))
    return jnp.concatenate(sums, axis=1)


def advance(src, cond, cool, film, heat, start, size, store):
    layers, count = src.shape[:2]
    rows = pl.ds(start, size)

    def tiles_of(l):
        if not 0 <= l < layers:
            return None
        return [src[l, j, pl.ds(start + 8, size), :] for j in range(count)]

    below, tiles, above = None, tiles_of(0), tiles_of(1)
    supply = None
    for l in range(layers):
        k = l // 2
        u = jnp.concatenate(tiles, axis=1)
        near = [jnp.concatenate(t, axis=1) for t in (below, above) if t is not None]
        if l % 2 == 0:
            supply = film[k : k + 1, :] * cool[k, rows, :]
        keep = (1.0 - 0.05 * len(near)) - film[k : k + 1, :]
        lateral = lateral_sum(src, l, tiles, start, size)
        new = u * keep + cond[l, rows, :] * (lateral - 4.0 * u)
        new = new + 0.05 * (near[0] + near[1] if len(near) == 2 else near[0])
        new = new + supply
        if l == 0:
            new = new + heat
        store(l, new)
        below, tiles, above = tiles, above, tiles_of(l + 2)


def pick(index, levels, count):
    values = [levels[i] for i in range(count)]
    bit = 1
    while len(values) > 1:
        if len(values) % 2:
            values.append(values[-1])
        odd = (index & bit) != 0
        values = [jnp.where(odd, values[i + 1], values[i]) for i in range(0, len(values), 2)]
        bit *= 2
    return values[0]


def kernel(
    n_flow, n_cross,
    u_hbm, c_hbm, cool_hbm, idx_hbm, lev_hbm, mask_hbm, inlet_hbm, gain_hbm,
    out, fluid, ends,
    u0, u1, cond, cool, idx, heat, lev, mask, inlet, gain,
    row_out, col_out, row_in, col_in, tot_out, tot_in,
    u_sem, big_sem, small_sem, halo_send, halo_recv, tot_send, tot_recv,
):
    layers, rows, width = u_hbm.shape
    chans = cool_hbm.shape[0]
    blocks = rows // 8
    per = LANES // layers
    groups = 4 if rows % (4 * STEP) == 0 else 1
    span = rows // groups
    lane_tiles = width // LANES
    edge_tiles = (0, lane_tiles - 1)
    me_f, me_c = lax.axis_index("flow"), lax.axis_index("cross")

    def loads(g):
        part = pl.ds(g * span, span)
        return [
            pltpu.make_async_copy(c_hbm.at[:, part], cond.at[:, part], big_sem.at[g, 1]),
            pltpu.make_async_copy(cool_hbm.at[:, part], cool.at[:, part], big_sem.at[g, 2]),
            pltpu.make_async_copy(idx_hbm.at[part], idx.at[part], big_sem.at[g, 3]),
        ]

    def load_u(g):
        return [
            pltpu.make_async_copy(
                u_hbm.at[:, pl.ds(g * span, span), pl.ds(j * LANES, LANES)],
                u0.at[:, j, pl.ds(8 + g * span, span)],
                u_sem.at[g, j],
            )
            for j in range(lane_tiles)
        ]

    small = [
        pltpu.make_async_copy(src, dst, small_sem.at[i])
        for i, (src, dst) in enumerate(
            [(lev_hbm, lev), (mask_hbm, mask), (inlet_hbm, inlet), (gain_hbm, gain)]
        )
    ]
    for g in range(groups):
        for one in load_u(g):
            one.start()
    for s in small:
        s.start()
    for g in range(groups):
        for one in loads(g):
            one.start()

    barrier = pltpu.get_barrier_semaphore()
    for d in range(1, n_flow):
        pl.semaphore_signal(
            barrier, inc=1, device_id=(lax.rem(me_f + d, n_flow), me_c), device_id_type=MESH
        )

    @pl.when(me_c > 0)
    def _():
        pl.semaphore_signal(barrier, inc=1, device_id=(me_f, me_c - 1), device_id_type=MESH)

    @pl.when(me_c < n_cross - 1)
    def _():
        pl.semaphore_signal(barrier, inc=1, device_id=(me_f, me_c + 1), device_id_type=MESH)

    zeros = jnp.zeros((layers, lane_tiles, 8, LANES), jnp.float32)
    for ref in (u0, u1):
        ref[:, :, 0:8, :] = zeros
        ref[:, :, rows + 8 : rows + 16, :] = zeros
    col_out[...] = jnp.zeros_like(col_out)
    tot_out[...] = jnp.zeros_like(tot_out)

    has = [me_f > 0, me_f < n_flow - 1, me_c > 0, me_c < n_cross - 1]
    peer = [
        (jnp.maximum(me_f - 1, 0), me_c),
        (jnp.minimum(me_f + 1, n_flow - 1), me_c),
        (me_f, jnp.maximum(me_c - 1, 0)),
        (me_f, jnp.minimum(me_c + 1, n_cross - 1)),
    ]

    def halo(turn, d):
        send, recv = (row_out, row_in) if d < 2 else (col_out, col_in)
        return pltpu.make_async_remote_copy(
            src_ref=send.at[turn, d % 2],
            dst_ref=recv.at[turn, 1 - d % 2],
            send_sem=halo_send.at[turn, d],
            recv_sem=halo_recv.at[turn, d + 1 - 2 * (d % 2)],
            device_id=peer[d],
            device_id_type=MESH,
        )

    def arrival(turn, d):
        recv = row_in if d < 2 else col_in
        return pltpu.make_async_remote_copy(
            src_ref=recv.at[turn, d % 2],
            dst_ref=recv.at[turn, d % 2],
            send_sem=halo_send.at[turn, d],
            recv_sem=halo_recv.at[turn, d],
            device_id=peer[d],
            device_id_type=MESH,
        )

    def send_halos(turn):
        for d in (2, 3, 0, 1):
            @pl.when(has[d])
            def _():
                halo(turn, d).start()

    def take_halos(turn):
        for d in range(4):
            @pl.when(has[d])
            def _():
                arrival(turn, d).wait_recv()

            @pl.when(jnp.logical_not(has[d]))
            def _():
                recv = row_in if d < 2 else col_in
                recv[turn, d % 2] = jnp.zeros(recv.shape[2:], jnp.float32)

    lane = lax.broadcasted_iota(jnp.int32, (8, LANES), 1)
    group = min(per, blocks)
    edge_cols = (pl.ds(0, LANES), pl.ds(width - LANES, LANES))
    is_layer = [lax.rem(lane, layers) == l for l in range(layers)]
    is_block = [lane // layers == i for i in range(group)]

    def turned(tile, shift):
        return pltpu.roll(tile, shift % LANES, 1) if shift % LANES else tile

    def pack_cols(turn, v, side, tiles_of):
        packed = jnp.zeros((8, LANES), jnp.float32)
        for i in range(group):
            joined = jnp.zeros((8, LANES), jnp.float32)
            for l, tile in enumerate(tiles_of(i)):
                joined = jnp.where(is_layer[l], turned(tile, i * layers + l + side), joined)
            packed = jnp.where(is_block[i], joined, packed)
        col_out[turn, side, pl.ds(pl.multiple_of(v * 8, 8), 8), :] = packed

    def fix_cols(turn, v, side, view):
        target = side * (LANES - 1)
        packed = col_in[turn, side, pl.ds(pl.multiple_of(v * 8, 8), 8), :]
        edge = lane == target

        def fixed(i):
            at = pl.multiple_of((v * group + i) * 8, 8)
            tiles = []
            for l in range(layers):
                beyond = jnp.where(edge, turned(packed, target - i * layers - l), 0.0)
                ref, where = view(side, l, at)
                tiles.append(ref[where] + beyond * cond[l, pl.ds(at, 8), edge_cols[side]])
            for l in range(layers):
                ref, where = view(side, l, at)
                ref[where] = tiles[l]
            return tiles

        return fixed

    def lane_tile(j):
        return pl.ds(j * LANES, LANES)

    def in_u1(side, l, at):
        return u1, (l, edge_tiles[side], pl.ds(at + 8, 8), slice(None))

    def in_out(side, l, at):
        return out, (l, pl.ds(at, 8), edge_cols[side])

    def beyond_rows(turn, l, side, row, j):
        return (
            cond[l, pl.ds(row, 1), lane_tile(j)] * row_in[turn, side, pl.ds(l, 1), lane_tile(j)]
        )

    def fix_rows(turn, final):
        for side, row in ((0, 0), (1, rows - 1)):
            done = []
            for l in range(layers):
                for j in range(lane_tiles):
                    if final:
                        ref, where = out, (l, pl.ds(row, 1), lane_tile(j))
                    else:
                        ref, where = u1, (l, j, pl.ds(row + 8, 1), slice(None))
                    done.append((ref, where, ref[where] + beyond_rows(turn, l, side, row, j)))
            for ref, where, value in done:
                ref[where] = value

    def pack_rows(turn, ref):
        for l in range(layers):
            for j in range(lane_tiles):
                for side, row in ((0, 8), (1, rows + 7)):
                    row_out[turn, side, pl.ds(l, 1), lane_tile(j)] = ref[l, j, pl.ds(row, 1), :]

    arrived = 0
    for v in range(blocks // group):
        while arrived * span < (v + 1) * group * 8:
            for one in load_u(arrived):
                one.wait()
            arrived += 1
        for side in range(2):
            pack_cols(
                0, v, side,
                lambda i: [
                    u0[l, edge_tiles[side], pl.ds((v * group + i) * 8 + 8, 8), :]
                    for l in range(layers)
                ],
            )
    pack_rows(0, u0)
    pl.semaphore_wait(barrier, n_flow - 1 + has[2].astype(jnp.int32) + has[3].astype(jnp.int32))
    send_halos(0)

    for s in small:
        s.wait()
    film = 0.08 * mask[...].astype(jnp.float32)

    for g in range(groups):
        for one in loads(g):
            one.wait()

        def first(i, _):
            for sub in range(0, STEP, 8):
                start = pl.multiple_of(g * span + i * STEP + sub, 8)
                warm = pick(idx[pl.ds(start, 8), :], lev, lev.shape[0])
                heat[pl.ds(start, 8), :] = warm

                def store(l, new):
                    for j in range(lane_tiles):
                        u1[l, j, pl.ds(start + 8, 8), :] = new[:, j * LANES : (j + 1) * LANES]

                advance(u0, cond, cool, film, warm, start, 8, store)
            return 0

        lax.fori_loop(0, span // STEP, first, 0)

    take_halos(0)
    fix_rows(0, False)

    def fix_first(v, _):
        for side in range(2):
            pack_cols(1, v, side, fix_cols(0, v, side, in_u1))
        return 0

    lax.fori_loop(0, blocks // group, fix_first, 0)
    pack_rows(1, u1)
    send_halos(1)

    def second(i, _):
        for sub in range(0, STEP, 8):
            start = pl.multiple_of(i * STEP + sub, 8)

            def store(l, new):
                out[l, pl.ds(start, 8), :] = new

            advance(u1, cond, cool, film, heat[pl.ds(start, 8), :], start, 8, store)
        return 0

    lax.fori_loop(0, rows // STEP, second, 0)
    take_halos(1)
    fix_rows(1, True)

    def fix_second(v, _):
        for side in range(2):
            fixed = fix_cols(1, v, side, in_out)
            for i in range(group):
                fixed(i)
        return 0

    lax.fori_loop(0, blocks // group, fix_second, 0)

    def take_up(i, sums):
        at = pl.ds(pl.multiple_of(i * CHUNK, CHUNK), CHUNK)
        new = []
        for k in range(chans):
            taken = film[k : k + 1, :] * (
                out[2 * k, at, :] + out[2 * k + 1, at, :] - 2.0 * cool[k, at, :]
            )
            fluid[k, at, :] = taken
            total = sums[k]
            for s in range(0, CHUNK, 8):
                total = total + taken[s : s + 8]
            new.append(total)
        return tuple(new)

    sums = lax.fori_loop(
        0, rows // CHUNK, take_up,
        tuple(jnp.zeros((8, width), jnp.float32) for _ in range(chans)),
    )
    for k in range(chans):
        tot_out[pl.ds(k, 1), :] = jnp.sum(sums[k], axis=0, keepdims=True)

    def carry(d):
        return pltpu.make_async_remote_copy(
            src_ref=tot_out,
            dst_ref=tot_in.at[d - 1],
            send_sem=tot_send.at[d - 1],
            recv_sem=tot_recv.at[d - 1],
            device_id=(lax.rem(me_f + d, n_flow), me_c),
            device_id_type=MESH,
        )

    for d in range(1, n_flow):
        @pl.when(me_f + d < n_flow)
        def _():
            carry(d).start()

    i_pos = lax.broadcasted_iota(jnp.int32, (rows, rows), 0)
    j_pos = lax.broadcasted_iota(jnp.int32, (rows, rows), 1)
    triangle = jnp.where(j_pos < i_pos, 1.0, jnp.where(j_pos == i_pos, 0.5, 0.0)).astype(
        jnp.bfloat16
    )
    part = 2 * LANES if width % (2 * LANES) == 0 else LANES
    for k in range(chans):
        for j in range(0, width, part):
            cols = pl.ds(j, part)
            taken = fluid[k, :, cols]
            high = taken.astype(jnp.bfloat16)
            low = (taken - high.astype(jnp.float32)).astype(jnp.bfloat16)
            fluid[k, :, cols] = jnp.dot(
                triangle, high, preferred_element_type=jnp.float32
            ) + jnp.dot(triangle, low, preferred_element_type=jnp.float32)

    for d in range(1, n_flow):
        @pl.when(me_f >= d)
        def _():
            carry(d).wait_recv()

        @pl.when(me_f < d)
        def _():
            tot_in[d - 1] = jnp.zeros(tot_in.shape[1:], jnp.float32)

    carried = tot_in[0]
    for d in range(2, n_flow):
        carried = carried + tot_in[d - 1]
    scale = gain[...] * (1.0 / (rows * n_flow))
    ends[0] = inlet[...] + scale * carried[:chans]
    ends[1] = scale

    for turn in range(2):
        for d in range(4):
            @pl.when(has[d])
            def _():
                halo(turn, d).wait_send()
    for d in range(1, n_flow):
        @pl.when(me_f + d < n_flow)
        def _():
            carry(d).wait_send()


def finish(solid, within, ends, out, fluid, held, solid_sem, fluid_sem):
    chans, rows, _ = within.shape
    whole = pltpu.make_async_copy(solid, out, solid_sem)
    whole.start()
    parts = []
    for k in range(chans):
        def march(i, _):
            at = pl.ds(pl.multiple_of(i * STEP, STEP), STEP)
            held[k, at, :] = ends[0, k : k + 1, :] + ends[1, k : k + 1, :] * within[k, at, :]
            return 0

        lax.fori_loop(0, rows // STEP, march, 0)
        parts.append(pltpu.make_async_copy(held.at[k], fluid.at[k], fluid_sem.at[k]))
        parts[k].start()
    whole.wait()
    for part in parts:
        part.wait()


def shards(
    solid_temp, conductance, coolant, power_index, power_levels, channel_mask, inlet, flow_gain
):
    n_flow, n_cross = lax.axis_size("flow"), lax.axis_size("cross")
    layers, rows, width = solid_temp.shape
    chans = coolant.shape[0]
    f32 = jnp.float32
    packed = pl.cdiv(rows // 8, LANES // layers) * 8
    totals = pl.cdiv(chans, 8) * 8
    scratch = [
        pltpu.VMEM((layers, width // LANES, rows + 16, LANES), f32),
        pltpu.VMEM((layers, width // LANES, rows + 16, LANES), f32),
        pltpu.VMEM((layers, rows, width), f32),
        pltpu.VMEM((chans, rows, width), f32),
        pltpu.VMEM((rows, width), jnp.int32),
        pltpu.VMEM((rows, width), f32),
        pltpu.SMEM(power_levels.shape, f32),
        pltpu.VMEM((chans, width), jnp.int32),
        pltpu.VMEM((chans, width), f32),
        pltpu.VMEM((chans, width), f32),
        pltpu.VMEM((2, 2, layers, width), f32),
        pltpu.VMEM((2, 2, packed, LANES), f32),
        pltpu.VMEM((2, 2, layers, width), f32),
        pltpu.VMEM((2, 2, packed, LANES), f32),
        pltpu.VMEM((totals, width), f32),
        pltpu.VMEM((n_flow - 1, totals, width), f32),
        pltpu.SemaphoreType.DMA((4, width // LANES)),
        pltpu.SemaphoreType.DMA((4, 4)),
        pltpu.SemaphoreType.DMA((4,)),
        pltpu.SemaphoreType.DMA((2, 4)),
        pltpu.SemaphoreType.DMA((2, 4)),
        pltpu.SemaphoreType.DMA((n_flow - 1,)),
        pltpu.SemaphoreType.DMA((n_flow - 1,)),
    ]
    cells = layers * rows * width
    limit = 57 * 1024 * 1024
    solid, within, ends = pl.pallas_call(
        functools.partial(kernel, n_flow, n_cross),
        out_shape=(
            pltpu.VMEM((layers, rows, width), f32),
            pltpu.VMEM((chans, rows, width), f32),
            pltpu.VMEM((2, chans, width), f32),
        ),
        in_specs=[pl.BlockSpec(memory_space=pltpu.HBM)] * 8,
        out_specs=(pl.BlockSpec(memory_space=pltpu.VMEM),) * 3,
        scratch_shapes=scratch,
        compiler_params=pltpu.CompilerParams(
            collective_id=0, has_side_effects=True, vmem_limit_bytes=limit
        ),
        cost_estimate=pl.CostEstimate(
            flops=40 * cells, bytes_accessed=11 * cells, transcendentals=0
        ),
    )(
        solid_temp, conductance, coolant, power_index, power_levels, channel_mask, inlet, flow_gain
    )
    return pl.pallas_call(
        finish,
        out_shape=(
            jax.ShapeDtypeStruct((layers, rows, width), f32),
            jax.ShapeDtypeStruct((chans, rows, width), f32),
        ),
        in_specs=[pl.BlockSpec(memory_space=pltpu.VMEM)] * 3,
        out_specs=(pl.BlockSpec(memory_space=pltpu.HBM),) * 2,
        scratch_shapes=[
            pltpu.VMEM((chans, rows, width), f32),
            pltpu.SemaphoreType.DMA,
            pltpu.SemaphoreType.DMA((chans,)),
        ],
        compiler_params=pltpu.CompilerParams(vmem_limit_bytes=16 * 1024 * 1024),
        cost_estimate=pl.CostEstimate(flops=cells, bytes_accessed=6 * cells, transcendentals=0),
    )(solid, within, ends)


def solution(mesh):
    return jax.shard_map(
        shards,
        mesh=mesh,
        in_specs=(
            P(None, "flow", "cross"),
            P(None, "flow", "cross"),
            P(None, "flow", "cross"),
            P("flow", "cross"),
            P(),
            P(None, "cross"),
            P(None, "cross"),
            P(None, "cross"),
        ),
        out_specs=(P(None, "flow", "cross"), P(None, "flow", "cross")),
        check_vma=False,
    )
```

```python
import functools

import jax
import jax.numpy as jnp
from jax import lax
from jax.experimental import pallas as pl
from jax.experimental.pallas import tpu as pltpu
from jax.sharding import PartitionSpec as P

MESH = pl.DeviceIdType.MESH
LANES = 128
CHUNK = 32
STEP = 64


def stencil(src, layer, start, size):
    count = src.shape[1]
    lane = lax.broadcasted_iota(jnp.int32, (size, LANES), 1)
    tiles = [src[layer, j, pl.ds(start + 8, size), :] for j in range(count)]
    none = jnp.zeros((size, LANES), jnp.float32)
    right_by_one = [none] + [pltpu.roll(t, 1, 1) for t in tiles]
    left_by_one = [pltpu.roll(t, LANES - 1, 1) for t in tiles] + [none]
    sums = []
    for j in range(count):
        left = jnp.where(lane == 0, right_by_one[j], right_by_one[j + 1])
        right = jnp.where(lane == LANES - 1, left_by_one[j + 1], left_by_one[j])
        above = src[layer, j, pl.ds(start + 7, size), :]
        below = src[layer, j, pl.ds(start + 9, size), :]
        sums.append((left + right) + (above + below))
    return jnp.concatenate(tiles, axis=1), jnp.concatenate(sums, axis=1)


def advance(src, cond, cool, film, heat, start, size, store):
    layers = src.shape[0]
    parts = [stencil(src, l, start, size) for l in range(layers)]
    rows = pl.ds(start, size)
    for l in range(layers):
        k = l // 2
        u, lateral = parts[l]
        near = [parts[m][0] for m in (l - 1, l + 1) if 0 <= m < layers]
        keep = (1.0 - 0.05 * len(near)) - film[k : k + 1, :]
        new = u * keep + cond[l, rows, :] * (lateral - 4.0 * u)
        new = new + 0.05 * (near[0] + near[1] if len(near) == 2 else near[0])
        new = new + film[k : k + 1, :] * cool[k, rows, :]
        if l == 0:
            new = new + heat
        store(l, new)


def pick(index, levels, count):
    values = [levels[i] for i in range(count)]
    bit = 1
    while len(values) > 1:
        if len(values) % 2:
            values.append(values[-1])
        odd = (index & bit) != 0
        values = [jnp.where(odd, values[i + 1], values[i]) for i in range(0, len(values), 2)]
        bit *= 2
    return values[0]


def kernel(
    n_flow, n_cross,
    u_hbm, c_hbm, cool_hbm, idx_hbm, lev_hbm, mask_hbm, inlet_hbm, gain_hbm,
    out, fluid, ends,
    u0, u1, cond, cool, idx, heat, lev, mask, inlet, gain,
    row_out, col_out, row_in, col_in, tot_out, tot_in,
    u_sem, big_sem, small_sem, halo_send, halo_recv, tot_send, tot_recv,
):
    layers, rows, width = u_hbm.shape
    chans = cool_hbm.shape[0]
    blocks = rows // 8
    per = LANES // layers
    groups = 4 if rows % (4 * CHUNK) == 0 else 1
    span = rows // groups
    step = next(n for n in (STEP, 32, 16, 8) if span % n == 0)
    lane_tiles = width // LANES
    edge_tiles = (0, lane_tiles - 1)
    me_f, me_c = lax.axis_index("flow"), lax.axis_index("cross")

    def loads(g):
        part = pl.ds(pl.multiple_of(g * span, span), span)
        return [
            pltpu.make_async_copy(c_hbm.at[:, part], cond.at[:, part], big_sem.at[g, 1]),
            pltpu.make_async_copy(cool_hbm.at[:, part], cool.at[:, part], big_sem.at[g, 2]),
            pltpu.make_async_copy(idx_hbm.at[part], idx.at[part], big_sem.at[g, 3]),
        ]

    def load_u(g):
        return [
            pltpu.make_async_copy(
                u_hbm.at[:, pl.ds(g * span, span), pl.ds(j * LANES, LANES)],
                u0.at[:, j, pl.ds(8 + g * span, span)],
                u_sem.at[g, j],
            )
            for j in range(lane_tiles)
        ]

    small = [
        pltpu.make_async_copy(src, dst, small_sem.at[i])
        for i, (src, dst) in enumerate(
            [(lev_hbm, lev), (mask_hbm, mask), (inlet_hbm, inlet), (gain_hbm, gain)]
        )
    ]
    lead = min(2, groups)
    for g in range(lead):
        for one in load_u(g):
            one.start()
    for one in small + loads(0):
        one.start()
    for g in range(lead, groups):
        for one in load_u(g):
            one.start()
    for g in range(1, groups):
        for one in loads(g):
            one.start()

    barrier = pltpu.get_barrier_semaphore()
    for d in range(1, n_flow):
        pl.semaphore_signal(
            barrier, inc=1, device_id=(lax.rem(me_f + d, n_flow), me_c), device_id_type=MESH
        )

    @pl.when(me_c > 0)
    def _():
        pl.semaphore_signal(barrier, inc=1, device_id=(me_f, me_c - 1), device_id_type=MESH)

    @pl.when(me_c < n_cross - 1)
    def _():
        pl.semaphore_signal(barrier, inc=1, device_id=(me_f, me_c + 1), device_id_type=MESH)

    zeros = jnp.zeros((layers, lane_tiles, 8, LANES), jnp.float32)
    for ref in (u0, u1):
        ref[:, :, 0:8, :] = zeros
        ref[:, :, rows + 8 : rows + 16, :] = zeros
    col_out[...] = jnp.zeros_like(col_out)
    tot_out[...] = jnp.zeros_like(tot_out)

    has = [me_f > 0, me_f < n_flow - 1, me_c > 0, me_c < n_cross - 1]
    peer = [
        (jnp.maximum(me_f - 1, 0), me_c),
        (jnp.minimum(me_f + 1, n_flow - 1), me_c),
        (me_f, jnp.maximum(me_c - 1, 0)),
        (me_f, jnp.minimum(me_c + 1, n_cross - 1)),
    ]

    def halo(turn, d):
        send, recv = (row_out, row_in) if d < 2 else (col_out, col_in)
        return pltpu.make_async_remote_copy(
            src_ref=send.at[turn, d % 2],
            dst_ref=recv.at[turn, 1 - d % 2],
            send_sem=halo_send.at[turn, d],
            recv_sem=halo_recv.at[turn, d + 1 - 2 * (d % 2)],
            device_id=peer[d],
            device_id_type=MESH,
        )

    def arrival(turn, d):
        recv = row_in if d < 2 else col_in
        return pltpu.make_async_remote_copy(
            src_ref=recv.at[turn, d % 2],
            dst_ref=recv.at[turn, d % 2],
            send_sem=halo_send.at[turn, d],
            recv_sem=halo_recv.at[turn, d],
            device_id=peer[d],
            device_id_type=MESH,
        )

    def send_halos(turn):
        for d in (2, 3, 0, 1):
            @pl.when(has[d])
            def _():
                halo(turn, d).start()

    def take_halos(turn):
        for d in range(4):
            @pl.when(has[d])
            def _():
                arrival(turn, d).wait_recv()

            @pl.when(jnp.logical_not(has[d]))
            def _():
                recv = row_in if d < 2 else col_in
                recv[turn, d % 2] = jnp.zeros(recv.shape[2:], jnp.float32)

    lane = lax.broadcasted_iota(jnp.int32, (8, LANES), 1)
    group = min(per, blocks)
    edge_cols = (pl.ds(0, LANES), pl.ds(width - LANES, LANES))
    is_layer = [lax.rem(lane, layers) == l for l in range(layers)]
    is_block = [lane // layers == i for i in range(group)]

    def turned(tile, shift):
        return pltpu.roll(tile, shift % LANES, 1) if shift % LANES else tile

    def pack_cols(turn, v, side, tiles_of):
        packed = jnp.zeros((8, LANES), jnp.float32)
        for i in range(group):
            joined = jnp.zeros((8, LANES), jnp.float32)
            for l, tile in enumerate(tiles_of(i)):
                joined = jnp.where(is_layer[l], turned(tile, i * layers + l + side), joined)
            packed = jnp.where(is_block[i], joined, packed)
        col_out[turn, side, pl.ds(pl.multiple_of(v * 8, 8), 8), :] = packed

    def fix_cols(turn, v, side, view):
        target = side * (LANES - 1)
        packed = col_in[turn, side, pl.ds(pl.multiple_of(v * 8, 8), 8), :]
        edge = lane == target

        def fixed(i):
            at = pl.multiple_of((v * group + i) * 8, 8)
            tiles = []
            for l in range(layers):
                beyond = jnp.where(edge, turned(packed, target - i * layers - l), 0.0)
                ref, where = view(side, l, at)
                tiles.append(ref[where] + beyond * cond[l, pl.ds(at, 8), edge_cols[side]])
            for l in range(layers):
                ref, where = view(side, l, at)
                ref[where] = tiles[l]
            return tiles

        return fixed

    def lane_tile(j):
        return pl.ds(j * LANES, LANES)

    def in_u1(side, l, at):
        return u1, (l, edge_tiles[side], pl.ds(at + 8, 8), slice(None))

    def in_out(side, l, at):
        return out, (l, pl.ds(at, 8), edge_cols[side])

    def beyond_rows(turn, l, side, row, j):
        return (
            cond[l, pl.ds(row, 1), lane_tile(j)] * row_in[turn, side, pl.ds(l, 1), lane_tile(j)]
        )

    def fix_rows(turn, final):
        for side, row in ((0, 0), (1, rows - 1)):
            done = []
            for l in range(layers):
                for j in range(lane_tiles):
                    if final:
                        ref, where = out, (l, pl.ds(row, 1), lane_tile(j))
                    else:
                        ref, where = u1, (l, j, pl.ds(row + 8, 1), slice(None))
                    done.append((ref, where, ref[where] + beyond_rows(turn, l, side, row, j)))
            for ref, where, value in done:
                ref[where] = value

    def pack_rows(turn, ref):
        for l in range(layers):
            for j in range(lane_tiles):
                for side, row in ((0, 8), (1, rows + 7)):
                    row_out[turn, side, pl.ds(l, 1), lane_tile(j)] = ref[l, j, pl.ds(row, 1), :]

    def first_step(g):
        for one in loads(g):
            one.wait()

        def first(i, _):
            start = pl.multiple_of(g * span + i * step, step)
            warm = pick(idx[pl.ds(start, step), :], lev, lev.shape[0])
            heat[pl.ds(start, step), :] = warm

            def store(l, new):
                for j in range(lane_tiles):
                    u1[l, j, pl.ds(start + 8, step), :] = new[:, j * LANES : (j + 1) * LANES]

            advance(u0, cond, cool, film, warm, start, step, store)
            return 0

        lax.fori_loop(0, span // step, first, 0)

    def pack_first(v, _):
        for side in range(2):
            pack_cols(
                0, v, side,
                lambda i: [
                    u0[
                        l,
                        edge_tiles[side],
                        pl.ds(pl.multiple_of((v * group + i) * 8 + 8, 8), 8),
                        :,
                    ]
                    for l in range(layers)
                ],
            )
        return 0

    for s in small:
        s.wait()
    film = 0.08 * mask[...].astype(jnp.float32)
    for g in range(lead):
        for one in load_u(g):
            one.wait()

    def first_group(g, _):
        @pl.when(g == lead - 1)
        def _():
            for h in range(lead, groups):
                for one in load_u(h):
                    one.wait()
            lax.fori_loop(0, blocks // group, pack_first, 0)
            pack_rows(0, u0)
            pl.semaphore_wait(
                barrier, n_flow - 1 + has[2].astype(jnp.int32) + has[3].astype(jnp.int32)
            )
            send_halos(0)

        first_step(g)
        return 0

    lax.fori_loop(0, groups, first_group, 0)

    take_halos(0)
    fix_rows(0, False)

    def fix_first(v, _):
        for side in range(2):
            pack_cols(1, v, side, fix_cols(0, v, side, in_u1))
        return 0

    lax.fori_loop(0, blocks // group, fix_first, 0)
    pack_rows(1, u1)
    send_halos(1)

    def second(i, _):
        start = pl.multiple_of(i * step, step)

        def store(l, new):
            out[l, pl.ds(start, step), :] = new

        advance(u1, cond, cool, film, heat[pl.ds(start, step), :], start, step, store)
        return 0

    lax.fori_loop(0, rows // step, second, 0)
    take_halos(1)
    fix_rows(1, True)

    def fix_second(v, _):
        for side in range(2):
            fixed = fix_cols(1, v, side, in_out)
            for i in range(group):
                fixed(i)
        return 0

    lax.fori_loop(0, blocks // group, fix_second, 0)

    def take_up(i, sums):
        at = pl.ds(pl.multiple_of(i * CHUNK, CHUNK), CHUNK)
        new = []
        for k in range(chans):
            taken = film[k : k + 1, :] * (
                out[2 * k, at, :] + out[2 * k + 1, at, :] - 2.0 * cool[k, at, :]
            )
            fluid[k, at, :] = taken
            total = sums[k]
            for s in range(0, CHUNK, 8):
                total = total + taken[s : s + 8]
            new.append(total)
        return tuple(new)

    sums = lax.fori_loop(
        0, rows // CHUNK, take_up,
        tuple(jnp.zeros((8, width), jnp.float32) for _ in range(chans)),
    )
    for k in range(chans):
        tot_out[pl.ds(k, 1), :] = jnp.sum(sums[k], axis=0, keepdims=True)

    def carry(d):
        return pltpu.make_async_remote_copy(
            src_ref=tot_out,
            dst_ref=tot_in.at[d - 1],
            send_sem=tot_send.at[d - 1],
            recv_sem=tot_recv.at[d - 1],
            device_id=(lax.rem(me_f + d, n_flow), me_c),
            device_id_type=MESH,
        )

    for d in range(1, n_flow):
        @pl.when(me_f + d < n_flow)
        def _():
            carry(d).start()

    i_pos = lax.broadcasted_iota(jnp.int32, (rows, rows), 0)
    j_pos = lax.broadcasted_iota(jnp.int32, (rows, rows), 1)
    triangle = jnp.where(j_pos < i_pos, 1.0, jnp.where(j_pos == i_pos, 0.5, 0.0)).astype(
        jnp.bfloat16
    )
    part = 2 * LANES if width % (2 * LANES) == 0 else LANES
    for k in range(chans):
        for j in range(0, width, part):
            cols = pl.ds(j, part)
            taken = fluid[k, :, cols]
            high = taken.astype(jnp.bfloat16)
            low = (taken - high.astype(jnp.float32)).astype(jnp.bfloat16)
            fluid[k, :, cols] = jnp.dot(
                triangle, high, preferred_element_type=jnp.float32
            ) + jnp.dot(triangle, low, preferred_element_type=jnp.float32)

    for d in range(1, n_flow):
        @pl.when(me_f >= d)
        def _():
            carry(d).wait_recv()

        @pl.when(me_f < d)
        def _():
            tot_in[d - 1] = jnp.zeros(tot_in.shape[1:], jnp.float32)

    carried = tot_in[0]
    for d in range(2, n_flow):
        carried = carried + tot_in[d - 1]
    scale = gain[...] * (1.0 / (rows * n_flow))
    ends[0] = inlet[...] + scale * carried[:chans]
    ends[1] = scale

    for turn in range(2):
        for d in range(4):
            @pl.when(has[d])
            def _():
                halo(turn, d).wait_send()
    for d in range(1, n_flow):
        @pl.when(me_f + d < n_flow)
        def _():
            carry(d).wait_send()


def finish(solid, within, ends, out, fluid, held, solid_sem, fluid_sem):
    chans, rows, _ = within.shape
    whole = pltpu.make_async_copy(solid, out, solid_sem)
    whole.start()
    parts = []
    for k in range(chans):
        def march(i, _):
            at = pl.ds(pl.multiple_of(i * CHUNK, CHUNK), CHUNK)
            held[k, at, :] = ends[0, k : k + 1, :] + ends[1, k : k + 1, :] * within[k, at, :]
            return 0

        lax.fori_loop(0, rows // CHUNK, march, 0)
        parts.append(pltpu.make_async_copy(held.at[k], fluid.at[k], fluid_sem.at[k]))
        parts[k].start()
    whole.wait()
    for part in parts:
        part.wait()


def shards(
    solid_temp, conductance, coolant, power_index, power_levels, channel_mask, inlet, flow_gain
):
    n_flow, n_cross = lax.axis_size("flow"), lax.axis_size("cross")
    layers, rows, width = solid_temp.shape
    chans = coolant.shape[0]
    f32 = jnp.float32
    packed = pl.cdiv(rows // 8, LANES // layers) * 8
    totals = pl.cdiv(chans, 8) * 8
    scratch = [
        pltpu.VMEM((layers, width // LANES, rows + 16, LANES), f32),
        pltpu.VMEM((layers, width // LANES, rows + 16, LANES), f32),
        pltpu.VMEM((layers, rows, width), f32),
        pltpu.VMEM((chans, rows, width), f32),
        pltpu.VMEM((rows, width), jnp.int32),
        pltpu.VMEM((rows, width), f32),
        pltpu.SMEM(power_levels.shape, f32),
        pltpu.VMEM((chans, width), jnp.int32),
        pltpu.VMEM((chans, width), f32),
        pltpu.VMEM((chans, width), f32),
        pltpu.VMEM((2, 2, layers, width), f32),
        pltpu.VMEM((2, 2, packed, LANES), f32),
        pltpu.VMEM((2, 2, layers, width), f32),
        pltpu.VMEM((2, 2, packed, LANES), f32),
        pltpu.VMEM((totals, width), f32),
        pltpu.VMEM((n_flow - 1, totals, width), f32),
        pltpu.SemaphoreType.DMA((4, width // LANES)),
        pltpu.SemaphoreType.DMA((4, 4)),
        pltpu.SemaphoreType.DMA((4,)),
        pltpu.SemaphoreType.DMA((2, 4)),
        pltpu.SemaphoreType.DMA((2, 4)),
        pltpu.SemaphoreType.DMA((n_flow - 1,)),
        pltpu.SemaphoreType.DMA((n_flow - 1,)),
    ]
    cells = layers * rows * width
    limit = 57 * 1024 * 1024
    solid, within, ends = pl.pallas_call(
        functools.partial(kernel, n_flow, n_cross),
        out_shape=(
            pltpu.VMEM((layers, rows, width), f32),
            pltpu.VMEM((chans, rows, width), f32),
            pltpu.VMEM((2, chans, width), f32),
        ),
        in_specs=[pl.BlockSpec(memory_space=pltpu.HBM)] * 8,
        out_specs=(pl.BlockSpec(memory_space=pltpu.VMEM),) * 3,
        scratch_shapes=scratch,
        compiler_params=pltpu.CompilerParams(
            collective_id=0, has_side_effects=True, vmem_limit_bytes=limit
        ),
        cost_estimate=pl.CostEstimate(
            flops=40 * cells, bytes_accessed=11 * cells, transcendentals=0
        ),
    )(
        solid_temp, conductance, coolant, power_index, power_levels, channel_mask, inlet, flow_gain
    )
    return pl.pallas_call(
        finish,
        out_shape=(
            jax.ShapeDtypeStruct((layers, rows, width), f32),
            jax.ShapeDtypeStruct((chans, rows, width), f32),
        ),
        in_specs=[pl.BlockSpec(memory_space=pltpu.VMEM)] * 3,
        out_specs=(pl.BlockSpec(memory_space=pltpu.HBM),) * 2,
        scratch_shapes=[
            pltpu.VMEM((chans, rows, width), f32),
            pltpu.SemaphoreType.DMA,
            pltpu.SemaphoreType.DMA((chans,)),
        ],
        compiler_params=pltpu.CompilerParams(vmem_limit_bytes=16 * 1024 * 1024),
        cost_estimate=pl.CostEstimate(flops=cells, bytes_accessed=6 * cells, transcendentals=0),
    )(solid, within, ends)


def solution(mesh):
    return jax.shard_map(
        shards,
        mesh=mesh,
        in_specs=(
            P(None, "flow", "cross"),
            P(None, "flow", "cross"),
            P(None, "flow", "cross"),
            P("flow", "cross"),
            P(),
            P(None, "cross"),
            P(None, "cross"),
            P(None, "cross"),
        ),
        out_specs=(P(None, "flow", "cross"), P(None, "flow", "cross")),
        check_vma=False,
    )
```

```python
import functools

import jax
import jax.numpy as jnp
from jax import lax
from jax.experimental import pallas as pl
from jax.experimental.pallas import tpu as pltpu
from jax.sharding import PartitionSpec as P

MESH = pl.DeviceIdType.MESH
LANES = 128
CHUNK = 32
STEP = 32


def stencil(src, layer, start, size):
    count = src.shape[1]
    lane = lax.broadcasted_iota(jnp.int32, (size, LANES), 1)
    tiles = [src[layer, j, pl.ds(start + 8, size), :] for j in range(count)]
    none = jnp.zeros((size, LANES), jnp.float32)
    right_by_one = [none] + [pltpu.roll(t, 1, 1) for t in tiles]
    left_by_one = [pltpu.roll(t, LANES - 1, 1) for t in tiles] + [none]
    sums = []
    for j in range(count):
        left = jnp.where(lane == 0, right_by_one[j], right_by_one[j + 1])
        right = jnp.where(lane == LANES - 1, left_by_one[j + 1], left_by_one[j])
        above = src[layer, j, pl.ds(start + 7, size), :]
        below = src[layer, j, pl.ds(start + 9, size), :]
        sums.append((left + right) + (above + below))
    return jnp.concatenate(tiles, axis=1), jnp.concatenate(sums, axis=1)


def advance(src, cond, cool, film, heat, start, size, store):
    layers = src.shape[0]
    parts = [stencil(src, l, start, size) for l in range(layers)]
    rows = pl.ds(start, size)
    for l in range(layers):
        k = l // 2
        u, lateral = parts[l]
        near = [parts[m][0] for m in (l - 1, l + 1) if 0 <= m < layers]
        keep = (1.0 - 0.05 * len(near)) - film[k : k + 1, :]
        new = u * keep + cond[l, rows, :] * (lateral - 4.0 * u)
        new = new + 0.05 * (near[0] + near[1] if len(near) == 2 else near[0])
        new = new + film[k : k + 1, :] * cool[k, rows, :]
        if l == 0:
            new = new + heat
        store(l, new)


def pick(index, levels, count):
    values = [levels[i] for i in range(count)]
    bit = 1
    while len(values) > 1:
        if len(values) % 2:
            values.append(values[-1])
        odd = (index & bit) != 0
        values = [jnp.where(odd, values[i + 1], values[i]) for i in range(0, len(values), 2)]
        bit *= 2
    return values[0]


def kernel(
    n_flow, n_cross,
    u_hbm, c_hbm, cool_hbm, idx_hbm, lev_hbm, mask_hbm, inlet_hbm, gain_hbm,
    out, fluid, ends,
    u0, u1, cond, cool, idx, heat, lev, mask, inlet, gain,
    row_out, col_out, row_in, col_in, tot_out, tot_in,
    u_sem, big_sem, small_sem, halo_send, halo_recv, tot_send, tot_recv,
):
    layers, rows, width = u_hbm.shape
    chans = cool_hbm.shape[0]
    blocks = rows // 8
    per = LANES // layers
    groups = 4 if rows % (4 * CHUNK) == 0 else 1
    span = rows // groups
    step = next(n for n in (STEP, 32, 16, 8) if span % n == 0)
    lane_tiles = width // LANES
    edge_tiles = (0, lane_tiles - 1)
    me_f, me_c = lax.axis_index("flow"), lax.axis_index("cross")

    def loads(g):
        part = pl.ds(pl.multiple_of(g * span, span), span)
        return [
            pltpu.make_async_copy(c_hbm.at[:, part], cond.at[:, part], big_sem.at[g, 1]),
            pltpu.make_async_copy(cool_hbm.at[:, part], cool.at[:, part], big_sem.at[g, 2]),
            pltpu.make_async_copy(idx_hbm.at[part], idx.at[part], big_sem.at[g, 3]),
        ]

    def load_u(g):
        return [
            pltpu.make_async_copy(
                u_hbm.at[:, pl.ds(g * span, span), pl.ds(j * LANES, LANES)],
                u0.at[:, j, pl.ds(8 + g * span, span)],
                u_sem.at[g, j],
            )
            for j in range(lane_tiles)
        ]

    small = [
        pltpu.make_async_copy(src, dst, small_sem.at[i])
        for i, (src, dst) in enumerate(
            [(lev_hbm, lev), (mask_hbm, mask), (inlet_hbm, inlet), (gain_hbm, gain)]
        )
    ]
    lead = min(2, groups)
    for g in range(lead):
        for one in load_u(g):
            one.start()
    for one in small + loads(0):
        one.start()
    for g in range(lead, groups):
        for one in load_u(g):
            one.start()
    for g in range(1, groups):
        for one in loads(g):
            one.start()

    barrier = pltpu.get_barrier_semaphore()
    for d in range(1, n_flow):
        pl.semaphore_signal(
            barrier, inc=1, device_id=(lax.rem(me_f + d, n_flow), me_c), device_id_type=MESH
        )

    @pl.when(me_c > 0)
    def _():
        pl.semaphore_signal(barrier, inc=1, device_id=(me_f, me_c - 1), device_id_type=MESH)

    @pl.when(me_c < n_cross - 1)
    def _():
        pl.semaphore_signal(barrier, inc=1, device_id=(me_f, me_c + 1), device_id_type=MESH)

    zeros = jnp.zeros((layers, lane_tiles, 8, LANES), jnp.float32)
    for ref in (u0, u1):
        ref[:, :, 0:8, :] = zeros
        ref[:, :, rows + 8 : rows + 16, :] = zeros
    col_out[...] = jnp.zeros_like(col_out)
    tot_out[...] = jnp.zeros_like(tot_out)

    has = [me_f > 0, me_f < n_flow - 1, me_c > 0, me_c < n_cross - 1]
    peer = [
        (jnp.maximum(me_f - 1, 0), me_c),
        (jnp.minimum(me_f + 1, n_flow - 1), me_c),
        (me_f, jnp.maximum(me_c - 1, 0)),
        (me_f, jnp.minimum(me_c + 1, n_cross - 1)),
    ]

    def halo(turn, d):
        send, recv = (row_out, row_in) if d < 2 else (col_out, col_in)
        return pltpu.make_async_remote_copy(
            src_ref=send.at[turn, d % 2],
            dst_ref=recv.at[turn, 1 - d % 2],
            send_sem=halo_send.at[turn, d],
            recv_sem=halo_recv.at[turn, d + 1 - 2 * (d % 2)],
            device_id=peer[d],
            device_id_type=MESH,
        )

    def arrival(turn, d):
        recv = row_in if d < 2 else col_in
        return pltpu.make_async_remote_copy(
            src_ref=recv.at[turn, d % 2],
            dst_ref=recv.at[turn, d % 2],
            send_sem=halo_send.at[turn, d],
            recv_sem=halo_recv.at[turn, d],
            device_id=peer[d],
            device_id_type=MESH,
        )

    def send_halos(turn):
        for d in (2, 3, 0, 1):
            @pl.when(has[d])
            def _():
                halo(turn, d).start()

    def take_halos(turn):
        for d in range(4):
            @pl.when(has[d])
            def _():
                arrival(turn, d).wait_recv()

            @pl.when(jnp.logical_not(has[d]))
            def _():
                recv = row_in if d < 2 else col_in
                recv[turn, d % 2] = jnp.zeros(recv.shape[2:], jnp.float32)

    lane = lax.broadcasted_iota(jnp.int32, (8, LANES), 1)
    group = min(per, blocks)
    edge_cols = (pl.ds(0, LANES), pl.ds(width - LANES, LANES))
    is_layer = [lax.rem(lane, layers) == l for l in range(layers)]
    is_block = [lane // layers == i for i in range(group)]

    def turned(tile, shift):
        return pltpu.roll(tile, shift % LANES, 1) if shift % LANES else tile

    def pack_cols(turn, v, side, tile_of):
        packed = jnp.zeros((8, LANES), jnp.float32)
        for i in range(group):
            joined = jnp.zeros((8, LANES), jnp.float32)
            for l in range(layers):
                joined = jnp.where(is_layer[l], turned(tile_of(i, l), i * layers + l + side), joined)
            packed = jnp.where(is_block[i], joined, packed)
        col_out[turn, side, pl.ds(pl.multiple_of(v * 8, 8), 8), :] = packed

    def fix_cols(turn, v, side, view):
        target = side * (LANES - 1)
        packed = col_in[turn, side, pl.ds(pl.multiple_of(v * 8, 8), 8), :]
        edge = lane == target
        tiles = {}
        for i in range(group):
            at = pl.multiple_of((v * group + i) * 8, 8)
            for l in range(layers):
                beyond = jnp.where(edge, turned(packed, target - i * layers - l), 0.0)
                ref, where = view(side, l, at)
                tile = ref[where] + beyond * cond[l, pl.ds(at, 8), edge_cols[side]]
                ref[where] = tile
                tiles[i, l] = tile
        return lambda i, l: tiles[i, l]

    def lane_tile(j):
        return pl.ds(j * LANES, LANES)

    def in_u1(side, l, at):
        return u1, (l, edge_tiles[side], pl.ds(at + 8, 8), slice(None))

    def in_out(side, l, at):
        return out, (l, pl.ds(at, 8), edge_cols[side])

    def beyond_rows(turn, l, side, row, j):
        return (
            cond[l, pl.ds(row, 1), lane_tile(j)] * row_in[turn, side, pl.ds(l, 1), lane_tile(j)]
        )

    def fix_rows(turn, final):
        for l in range(layers):
            for side, row in ((0, 0), (1, rows - 1)):
                for j in range(lane_tiles):
                    term = beyond_rows(turn, l, side, row, j)
                    if final:
                        where = (l, pl.ds(row, 1), lane_tile(j))
                        out[where] = out[where] + term
                    else:
                        where = (l, j, pl.ds(row + 8, 1), slice(None))
                        u1[where] = u1[where] + term

    def pack_rows(turn, ref):
        for l in range(layers):
            for j in range(lane_tiles):
                for side, row in ((0, 8), (1, rows + 7)):
                    row_out[turn, side, pl.ds(l, 1), lane_tile(j)] = ref[l, j, pl.ds(row, 1), :]

    def first_step(g):
        for one in loads(g):
            one.wait()

        def first(i, _):
            start = pl.multiple_of(g * span + i * step, step)
            warm = pick(idx[pl.ds(start, step), :], lev, lev.shape[0])
            heat[pl.ds(start, step), :] = warm

            def store(l, new):
                for j in range(lane_tiles):
                    u1[l, j, pl.ds(start + 8, step), :] = new[:, j * LANES : (j + 1) * LANES]

            advance(u0, cond, cool, film, warm, start, step, store)
            return 0

        lax.fori_loop(0, span // step, first, 0)

    def pack_first(v, _):
        for side in range(2):
            pack_cols(
                0, v, side,
                lambda i, l: u0[
                    l,
                    edge_tiles[side],
                    pl.ds(pl.multiple_of((v * group + i) * 8 + 8, 8), 8),
                    :,
                ],
            )
        return 0

    for s in small:
        s.wait()
    film = 0.08 * mask[...].astype(jnp.float32)
    for g in range(lead):
        for one in load_u(g):
            one.wait()

    def first_group(g, _):
        @pl.when(g == lead - 1)
        def _():
            for h in range(lead, groups):
                for one in load_u(h):
                    one.wait()
            lax.fori_loop(0, blocks // group, pack_first, 0)
            pack_rows(0, u0)
            pl.semaphore_wait(
                barrier, n_flow - 1 + has[2].astype(jnp.int32) + has[3].astype(jnp.int32)
            )
            send_halos(0)

        first_step(g)
        return 0

    lax.fori_loop(0, groups, first_group, 0)

    take_halos(0)
    fix_rows(0, False)

    def fix_first(v, _):
        for side in range(2):
            pack_cols(1, v, side, fix_cols(0, v, side, in_u1))
        return 0

    lax.fori_loop(0, blocks // group, fix_first, 0)
    pack_rows(1, u1)
    send_halos(1)

    def second(i, _):
        start = pl.multiple_of(i * step, step)

        def store(l, new):
            out[l, pl.ds(start, step), :] = new

        advance(u1, cond, cool, film, heat[pl.ds(start, step), :], start, step, store)
        return 0

    lax.fori_loop(0, rows // step, second, 0)
    take_halos(1)
    fix_rows(1, True)

    def fix_second(v, _):
        for side in range(2):
            fix_cols(1, v, side, in_out)
        return 0

    lax.fori_loop(0, blocks // group, fix_second, 0)

    def take_up(i, sums):
        at = pl.ds(pl.multiple_of(i * CHUNK, CHUNK), CHUNK)
        new = []
        for k in range(chans):
            taken = film[k : k + 1, :] * (
                out[2 * k, at, :] + out[2 * k + 1, at, :] - 2.0 * cool[k, at, :]
            )
            fluid[k, at, :] = taken
            total = sums[k]
            for s in range(0, CHUNK, 8):
                total = total + taken[s : s + 8]
            new.append(total)
        return tuple(new)

    sums = lax.fori_loop(
        0, rows // CHUNK, take_up,
        tuple(jnp.zeros((8, width), jnp.float32) for _ in range(chans)),
    )
    for k in range(chans):
        tot_out[pl.ds(k, 1), :] = jnp.sum(sums[k], axis=0, keepdims=True)

    def carry(d):
        return pltpu.make_async_remote_copy(
            src_ref=tot_out,
            dst_ref=tot_in.at[d - 1],
            send_sem=tot_send.at[d - 1],
            recv_sem=tot_recv.at[d - 1],
            device_id=(lax.rem(me_f + d, n_flow), me_c),
            device_id_type=MESH,
        )

    for d in range(1, n_flow):
        @pl.when(me_f + d < n_flow)
        def _():
            carry(d).start()

    i_pos = lax.broadcasted_iota(jnp.int32, (rows, rows), 0)
    j_pos = lax.broadcasted_iota(jnp.int32, (rows, rows), 1)
    triangle = jnp.where(j_pos < i_pos, 1.0, jnp.where(j_pos == i_pos, 0.5, 0.0)).astype(
        jnp.bfloat16
    )
    part = 2 * LANES if width % (2 * LANES) == 0 else LANES
    for k in range(chans):
        for j in range(0, width, part):
            cols = pl.ds(j, part)
            taken = fluid[k, :, cols]
            high = taken.astype(jnp.bfloat16)
            low = (taken - high.astype(jnp.float32)).astype(jnp.bfloat16)
            fluid[k, :, cols] = jnp.dot(
                triangle, high, preferred_element_type=jnp.float32
            ) + jnp.dot(triangle, low, preferred_element_type=jnp.float32)

    for d in range(1, n_flow):
        @pl.when(me_f >= d)
        def _():
            carry(d).wait_recv()

        @pl.when(me_f < d)
        def _():
            tot_in[d - 1] = jnp.zeros(tot_in.shape[1:], jnp.float32)

    carried = tot_in[0]
    for d in range(2, n_flow):
        carried = carried + tot_in[d - 1]
    scale = gain[...] * (1.0 / (rows * n_flow))
    ends[0] = inlet[...] + scale * carried[:chans]
    ends[1] = scale

    for turn in range(2):
        for d in range(4):
            @pl.when(has[d])
            def _():
                halo(turn, d).wait_send()
    for d in range(1, n_flow):
        @pl.when(me_f + d < n_flow)
        def _():
            carry(d).wait_send()


def finish(solid, within, ends, out, fluid, held, solid_sem, fluid_sem):
    chans, rows, _ = within.shape
    parts = [
        pltpu.make_async_copy(solid.at[l], out.at[l], solid_sem.at[l])
        for l in range(solid.shape[0])
    ]
    for part in parts:
        part.start()
    for k in range(chans):
        def march(i, _):
            at = pl.ds(pl.multiple_of(i * CHUNK, CHUNK), CHUNK)
            held[k, at, :] = ends[0, k : k + 1, :] + ends[1, k : k + 1, :] * within[k, at, :]
            return 0

        lax.fori_loop(0, rows // CHUNK, march, 0)
        parts.append(pltpu.make_async_copy(held.at[k], fluid.at[k], fluid_sem.at[k]))
        parts[-1].start()
    for part in parts:
        part.wait()


def shards(
    solid_temp, conductance, coolant, power_index, power_levels, channel_mask, inlet, flow_gain
):
    n_flow, n_cross = lax.axis_size("flow"), lax.axis_size("cross")
    layers, rows, width = solid_temp.shape
    chans = coolant.shape[0]
    f32 = jnp.float32
    packed = pl.cdiv(rows // 8, LANES // layers) * 8
    totals = pl.cdiv(chans, 8) * 8
    scratch = [
        pltpu.VMEM((layers, width // LANES, rows + 16, LANES), f32),
        pltpu.VMEM((layers, width // LANES, rows + 16, LANES), f32),
        pltpu.VMEM((layers, rows, width), f32),
        pltpu.VMEM((chans, rows, width), f32),
        pltpu.VMEM((rows, width), jnp.int32),
        pltpu.VMEM((rows, width), f32),
        pltpu.SMEM(power_levels.shape, f32),
        pltpu.VMEM((chans, width), jnp.int32),
        pltpu.VMEM((chans, width), f32),
        pltpu.VMEM((chans, width), f32),
        pltpu.VMEM((2, 2, layers, width), f32),
        pltpu.VMEM((2, 2, packed, LANES), f32),
        pltpu.VMEM((2, 2, layers, width), f32),
        pltpu.VMEM((2, 2, packed, LANES), f32),
        pltpu.VMEM((totals, width), f32),
        pltpu.VMEM((n_flow - 1, totals, width), f32),
        pltpu.SemaphoreType.DMA((4, width // LANES)),
        pltpu.SemaphoreType.DMA((4, 4)),
        pltpu.SemaphoreType.DMA((4,)),
        pltpu.SemaphoreType.DMA((2, 4)),
        pltpu.SemaphoreType.DMA((2, 4)),
        pltpu.SemaphoreType.DMA((n_flow - 1,)),
        pltpu.SemaphoreType.DMA((n_flow - 1,)),
    ]
    cells = layers * rows * width
    limit = 57 * 1024 * 1024
    solid, within, ends = pl.pallas_call(
        functools.partial(kernel, n_flow, n_cross),
        out_shape=(
            pltpu.VMEM((layers, rows, width), f32),
            pltpu.VMEM((chans, rows, width), f32),
            pltpu.VMEM((2, chans, width), f32),
        ),
        in_specs=[pl.BlockSpec(memory_space=pltpu.HBM)] * 8,
        out_specs=(pl.BlockSpec(memory_space=pltpu.VMEM),) * 3,
        scratch_shapes=scratch,
        compiler_params=pltpu.CompilerParams(
            collective_id=0, has_side_effects=True, vmem_limit_bytes=limit
        ),
        cost_estimate=pl.CostEstimate(
            flops=40 * cells, bytes_accessed=11 * cells, transcendentals=0
        ),
    )(
        solid_temp, conductance, coolant, power_index, power_levels, channel_mask, inlet, flow_gain
    )
    return pl.pallas_call(
        finish,
        out_shape=(
            jax.ShapeDtypeStruct((layers, rows, width), f32),
            jax.ShapeDtypeStruct((chans, rows, width), f32),
        ),
        in_specs=[pl.BlockSpec(memory_space=pltpu.VMEM)] * 3,
        out_specs=(pl.BlockSpec(memory_space=pltpu.HBM),) * 2,
        scratch_shapes=[
            pltpu.VMEM((chans, rows, width), f32),
            pltpu.SemaphoreType.DMA((layers,)),
            pltpu.SemaphoreType.DMA((chans,)),
        ],
        compiler_params=pltpu.CompilerParams(vmem_limit_bytes=16 * 1024 * 1024),
        cost_estimate=pl.CostEstimate(flops=cells, bytes_accessed=6 * cells, transcendentals=0),
    )(solid, within, ends)


def solution(mesh):
    return jax.shard_map(
        shards,
        mesh=mesh,
        in_specs=(
            P(None, "flow", "cross"),
            P(None, "flow", "cross"),
            P(None, "flow", "cross"),
            P("flow", "cross"),
            P(),
            P(None, "cross"),
            P(None, "cross"),
            P(None, "cross"),
        ),
        out_specs=(P(None, "flow", "cross"), P(None, "flow", "cross")),
        check_vma=False,
    )
```

```python
import functools

import jax
import jax.numpy as jnp
from jax import lax
from jax.experimental import pallas as pl
from jax.experimental.pallas import tpu as pltpu
from jax.sharding import PartitionSpec as P

MESH = pl.DeviceIdType.MESH
LANES = 128
CHUNK = 32
STEP = 32


def stencil(src, layer, start, size):
    count = src.shape[1]
    lane = lax.broadcasted_iota(jnp.int32, (size, LANES), 1)
    tiles = [src[layer, j, pl.ds(start + 8, size), :] for j in range(count)]
    none = jnp.zeros((size, LANES), jnp.float32)
    right_by_one = [none] + [pltpu.roll(t, 1, 1) for t in tiles]
    left_by_one = [pltpu.roll(t, LANES - 1, 1) for t in tiles] + [none]
    sums = []
    for j in range(count):
        left = jnp.where(lane == 0, right_by_one[j], right_by_one[j + 1])
        right = jnp.where(lane == LANES - 1, left_by_one[j + 1], left_by_one[j])
        above = src[layer, j, pl.ds(start + 7, size), :]
        below = src[layer, j, pl.ds(start + 9, size), :]
        sums.append((left + right) + (above + below))
    return jnp.concatenate(tiles, axis=1), jnp.concatenate(sums, axis=1)


def advance(src, cond, cool, film, heat, start, size, store):
    layers = src.shape[0]
    parts = [stencil(src, l, start, size) for l in range(layers)]
    rows = pl.ds(start, size)
    for l in range(layers):
        k = l // 2
        u, lateral = parts[l]
        near = [parts[m][0] for m in (l - 1, l + 1) if 0 <= m < layers]
        keep = (1.0 - 0.05 * len(near)) - film[k : k + 1, :]
        new = u * keep + cond[l, rows, :] * (lateral - 4.0 * u)
        new = new + 0.05 * (near[0] + near[1] if len(near) == 2 else near[0])
        new = new + film[k : k + 1, :] * cool[k, rows, :]
        if l == 0:
            new = new + heat
        store(l, new)


def pick(index, levels, count):
    values = [levels[i] for i in range(count)]
    bit = 1
    while len(values) > 1:
        if len(values) % 2:
            values.append(values[-1])
        odd = (index & bit) != 0
        values = [jnp.where(odd, values[i + 1], values[i]) for i in range(0, len(values), 2)]
        bit *= 2
    return values[0]


def kernel(
    n_flow, n_cross,
    u_hbm, c_hbm, cool_hbm, idx_hbm, lev_hbm, mask_hbm, inlet_hbm, gain_hbm,
    out, fluid, ends,
    u0, u1, cond, cool, idx, heat, lev, mask, inlet, gain,
    row_out, col_out, row_in, col_in, tot_out, tot_in,
    u_sem, big_sem, small_sem, halo_send, halo_recv, tot_send, tot_recv,
):
    layers, rows, width = u_hbm.shape
    chans = cool_hbm.shape[0]
    blocks = rows // 8
    per = LANES // layers
    groups = 4 if rows % (4 * CHUNK) == 0 else 1
    span = rows // groups
    step = next(n for n in (STEP, 32, 16, 8) if span % n == 0)
    lane_tiles = width // LANES
    edge_tiles = (0, lane_tiles - 1)
    me_f, me_c = lax.axis_index("flow"), lax.axis_index("cross")

    def loads(g):
        part = pl.ds(pl.multiple_of(g * span, span), span)
        return [
            pltpu.make_async_copy(c_hbm.at[:, part], cond.at[:, part], big_sem.at[g, 1]),
            pltpu.make_async_copy(cool_hbm.at[:, part], cool.at[:, part], big_sem.at[g, 2]),
            pltpu.make_async_copy(idx_hbm.at[part], idx.at[part], big_sem.at[g, 3]),
        ]

    def load_u(g):
        return [
            pltpu.make_async_copy(
                u_hbm.at[:, pl.ds(g * span, span), pl.ds(j * LANES, LANES)],
                u0.at[:, j, pl.ds(8 + g * span, span)],
                u_sem.at[g, j],
            )
            for j in range(lane_tiles)
        ]

    small = [
        pltpu.make_async_copy(src, dst, small_sem.at[i])
        for i, (src, dst) in enumerate(
            [(lev_hbm, lev), (mask_hbm, mask), (inlet_hbm, inlet), (gain_hbm, gain)]
        )
    ]
    lead = min(2, groups)
    for g in range(lead):
        for one in load_u(g):
            one.start()
    for one in small + loads(0):
        one.start()
    for g in range(lead, groups):
        for one in load_u(g):
            one.start()
    for g in range(1, groups):
        for one in loads(g):
            one.start()

    barrier = pltpu.get_barrier_semaphore()
    for d in range(1, n_flow):
        pl.semaphore_signal(
            barrier, inc=1, device_id=(lax.rem(me_f + d, n_flow), me_c), device_id_type=MESH
        )

    @pl.when(me_c > 0)
    def _():
        pl.semaphore_signal(barrier, inc=1, device_id=(me_f, me_c - 1), device_id_type=MESH)

    @pl.when(me_c < n_cross - 1)
    def _():
        pl.semaphore_signal(barrier, inc=1, device_id=(me_f, me_c + 1), device_id_type=MESH)

    zeros = jnp.zeros((layers, lane_tiles, 8, LANES), jnp.float32)
    for ref in (u0, u1):
        ref[:, :, 0:8, :] = zeros
        ref[:, :, rows + 8 : rows + 16, :] = zeros
    col_out[...] = jnp.zeros_like(col_out)
    tot_out[...] = jnp.zeros_like(tot_out)

    has = [me_f > 0, me_f < n_flow - 1, me_c > 0, me_c < n_cross - 1]
    peer = [
        (jnp.maximum(me_f - 1, 0), me_c),
        (jnp.minimum(me_f + 1, n_flow - 1), me_c),
        (me_f, jnp.maximum(me_c - 1, 0)),
        (me_f, jnp.minimum(me_c + 1, n_cross - 1)),
    ]

    def halo(turn, d):
        send, recv = (row_out, row_in) if d < 2 else (col_out, col_in)
        return pltpu.make_async_remote_copy(
            src_ref=send.at[turn, d % 2],
            dst_ref=recv.at[turn, 1 - d % 2],
            send_sem=halo_send.at[turn, d],
            recv_sem=halo_recv.at[turn, d + 1 - 2 * (d % 2)],
            device_id=peer[d],
            device_id_type=MESH,
        )

    def arrival(turn, d):
        recv = row_in if d < 2 else col_in
        return pltpu.make_async_remote_copy(
            src_ref=recv.at[turn, d % 2],
            dst_ref=recv.at[turn, d % 2],
            send_sem=halo_send.at[turn, d],
            recv_sem=halo_recv.at[turn, d],
            device_id=peer[d],
            device_id_type=MESH,
        )

    def send_halos(turn):
        for d in (2, 3, 0, 1):
            @pl.when(has[d])
            def _():
                halo(turn, d).start()

    def take_halos(turn):
        for d in range(4):
            @pl.when(has[d])
            def _():
                arrival(turn, d).wait_recv()

            @pl.when(jnp.logical_not(has[d]))
            def _():
                recv = row_in if d < 2 else col_in
                recv[turn, d % 2] = jnp.zeros(recv.shape[2:], jnp.float32)

    lane = lax.broadcasted_iota(jnp.int32, (8, LANES), 1)
    group = min(per, blocks)
    edge_cols = (pl.ds(0, LANES), pl.ds(width - LANES, LANES))
    is_layer = [lax.rem(lane, layers) == l for l in range(layers)]
    is_block = [lane // layers == i for i in range(group)]

    def turned(tile, shift):
        return pltpu.roll(tile, shift % LANES, 1) if shift % LANES else tile

    def pack_cols(turn, v, side, tile_of):
        packed = jnp.zeros((8, LANES), jnp.float32)
        for i in range(group):
            joined = jnp.zeros((8, LANES), jnp.float32)
            for l in range(layers):
                joined = jnp.where(is_layer[l], turned(tile_of(i, l), i * layers + l + side), joined)
            packed = jnp.where(is_block[i], joined, packed)
        col_out[turn, side, pl.ds(pl.multiple_of(v * 8, 8), 8), :] = packed

    def fix_cols(turn, v, side, view):
        target = side * (LANES - 1)
        packed = col_in[turn, side, pl.ds(pl.multiple_of(v * 8, 8), 8), :]
        edge = lane == target
        tiles = {}
        for i in range(group):
            at = pl.multiple_of((v * group + i) * 8, 8)
            for l in range(layers):
                beyond = jnp.where(edge, turned(packed, target - i * layers - l), 0.0)
                ref, where = view(side, l, at)
                tile = ref[where] + beyond * cond[l, pl.ds(at, 8), edge_cols[side]]
                tiles[i, l] = tile

        def keep():
            for i in range(group):
                at = pl.multiple_of((v * group + i) * 8, 8)
                for l in range(layers):
                    ref, where = view(side, l, at)
                    ref[where] = tiles[i, l]

        return (lambda i, l: tiles[i, l]), keep

    def lane_tile(j):
        return pl.ds(j * LANES, LANES)

    def in_u1(side, l, at):
        return u1, (l, edge_tiles[side], pl.ds(at + 8, 8), slice(None))

    def in_out(side, l, at):
        return out, (l, pl.ds(at, 8), edge_cols[side])

    def beyond_rows(turn, l, side, row, j):
        return (
            cond[l, pl.ds(row, 1), lane_tile(j)] * row_in[turn, side, pl.ds(l, 1), lane_tile(j)]
        )

    def fix_rows(turn, final):
        for l in range(layers):
            for side, row in ((0, 0), (1, rows - 1)):
                for j in range(lane_tiles):
                    term = beyond_rows(turn, l, side, row, j)
                    if final:
                        where = (l, pl.ds(row, 1), lane_tile(j))
                        out[where] = out[where] + term
                    else:
                        where = (l, j, pl.ds(row + 8, 1), slice(None))
                        u1[where] = u1[where] + term

    def pack_rows(turn, ref):
        for l in range(layers):
            for j in range(lane_tiles):
                for side, row in ((0, 8), (1, rows + 7)):
                    row_out[turn, side, pl.ds(l, 1), lane_tile(j)] = ref[l, j, pl.ds(row, 1), :]

    def first_step(g):
        for one in loads(g):
            one.wait()

        def first(i, _):
            start = pl.multiple_of(g * span + i * step, step)
            warm = pick(idx[pl.ds(start, step), :], lev, lev.shape[0])
            heat[pl.ds(start, step), :] = warm

            def store(l, new):
                for j in range(lane_tiles):
                    u1[l, j, pl.ds(start + 8, step), :] = new[:, j * LANES : (j + 1) * LANES]

            advance(u0, cond, cool, film, warm, start, step, store)
            return 0

        lax.fori_loop(0, span // step, first, 0)

    def pack_first(v, _):
        for side in range(2):
            pack_cols(
                0, v, side,
                lambda i, l: u0[
                    l,
                    edge_tiles[side],
                    pl.ds(pl.multiple_of((v * group + i) * 8 + 8, 8), 8),
                    :,
                ],
            )
        return 0

    for s in small:
        s.wait()
    film = 0.08 * mask[...].astype(jnp.float32)
    for g in range(lead):
        for one in load_u(g):
            one.wait()

    def first_group(g, _):
        @pl.when(g == lead - 1)
        def _():
            for h in range(lead, groups):
                for one in load_u(h):
                    one.wait()
            lax.fori_loop(0, blocks // group, pack_first, 0)
            pack_rows(0, u0)
            pl.semaphore_wait(
                barrier, n_flow - 1 + has[2].astype(jnp.int32) + has[3].astype(jnp.int32)
            )
            send_halos(0)

        first_step(g)
        return 0

    lax.fori_loop(0, groups, first_group, 0)

    take_halos(0)
    fix_rows(0, False)

    def fix_first(v, _):
        for side in range(2):
            tile_of, keep = fix_cols(0, v, side, in_u1)
            pack_cols(1, v, side, tile_of)
            keep()
        return 0

    lax.fori_loop(0, blocks // group, fix_first, 0)
    pack_rows(1, u1)
    send_halos(1)

    def second(i, _):
        start = pl.multiple_of(i * step, step)

        def store(l, new):
            out[l, pl.ds(start, step), :] = new

        advance(u1, cond, cool, film, heat[pl.ds(start, step), :], start, step, store)
        return 0

    lax.fori_loop(0, rows // step, second, 0)
    take_halos(1)
    fix_rows(1, True)

    def fix_second(v, _):
        for side in range(2):
            fix_cols(1, v, side, in_out)[1]()
        return 0

    lax.fori_loop(0, blocks // group, fix_second, 0)

    def take_up(i, sums):
        at = pl.ds(pl.multiple_of(i * CHUNK, CHUNK), CHUNK)
        new = []
        for k in range(chans):
            taken = film[k : k + 1, :] * (
                out[2 * k, at, :] + out[2 * k + 1, at, :] - 2.0 * cool[k, at, :]
            )
            fluid[k, at, :] = taken
            total = sums[k]
            for s in range(0, CHUNK, 8):
                total = total + taken[s : s + 8]
            new.append(total)
        return tuple(new)

    sums = lax.fori_loop(
        0, rows // CHUNK, take_up,
        tuple(jnp.zeros((8, width), jnp.float32) for _ in range(chans)),
    )
    for k in range(chans):
        tot_out[pl.ds(k, 1), :] = jnp.sum(sums[k], axis=0, keepdims=True)

    def carry(d):
        return pltpu.make_async_remote_copy(
            src_ref=tot_out,
            dst_ref=tot_in.at[d - 1],
            send_sem=tot_send.at[d - 1],
            recv_sem=tot_recv.at[d - 1],
            device_id=(lax.rem(me_f + d, n_flow), me_c),
            device_id_type=MESH,
        )

    for d in range(1, n_flow):
        @pl.when(me_f + d < n_flow)
        def _():
            carry(d).start()

    i_pos = lax.broadcasted_iota(jnp.int32, (rows, rows), 0)
    j_pos = lax.broadcasted_iota(jnp.int32, (rows, rows), 1)
    triangle = jnp.where(j_pos < i_pos, 1.0, jnp.where(j_pos == i_pos, 0.5, 0.0)).astype(
        jnp.bfloat16
    )
    part = 2 * LANES if width % (2 * LANES) == 0 else LANES
    for k in range(chans):
        for j in range(0, width, part):
            cols = pl.ds(j, part)
            taken = fluid[k, :, cols]
            high = taken.astype(jnp.bfloat16)
            low = (taken - high.astype(jnp.float32)).astype(jnp.bfloat16)
            fluid[k, :, cols] = jnp.dot(
                triangle, high, preferred_element_type=jnp.float32
            ) + jnp.dot(triangle, low, preferred_element_type=jnp.float32)

    for d in range(1, n_flow):
        @pl.when(me_f >= d)
        def _():
            carry(d).wait_recv()

        @pl.when(me_f < d)
        def _():
            tot_in[d - 1] = jnp.zeros(tot_in.shape[1:], jnp.float32)

    carried = tot_in[0]
    for d in range(2, n_flow):
        carried = carried + tot_in[d - 1]
    scale = gain[...] * (1.0 / (rows * n_flow))
    ends[0] = inlet[...] + scale * carried[:chans]
    ends[1] = scale

    for turn in range(2):
        for d in range(4):
            @pl.when(has[d])
            def _():
                halo(turn, d).wait_send()
    for d in range(1, n_flow):
        @pl.when(me_f + d < n_flow)
        def _():
            carry(d).wait_send()


def finish(solid, within, ends, out, fluid, held, solid_sem, fluid_sem):
    chans, rows, _ = within.shape
    parts = [
        pltpu.make_async_copy(solid.at[l], out.at[l], solid_sem.at[l])
        for l in range(solid.shape[0])
    ]
    for part in parts:
        part.start()
    for k in range(chans):
        def march(i, _):
            at = pl.ds(pl.multiple_of(i * CHUNK, CHUNK), CHUNK)
            held[k, at, :] = ends[0, k : k + 1, :] + ends[1, k : k + 1, :] * within[k, at, :]
            return 0

        lax.fori_loop(0, rows // CHUNK, march, 0)
        parts.append(pltpu.make_async_copy(held.at[k], fluid.at[k], fluid_sem.at[k]))
        parts[-1].start()
    for part in parts:
        part.wait()


def shards(
    solid_temp, conductance, coolant, power_index, power_levels, channel_mask, inlet, flow_gain
):
    n_flow, n_cross = lax.axis_size("flow"), lax.axis_size("cross")
    layers, rows, width = solid_temp.shape
    chans = coolant.shape[0]
    f32 = jnp.float32
    packed = pl.cdiv(rows // 8, LANES // layers) * 8
    totals = pl.cdiv(chans, 8) * 8
    scratch = [
        pltpu.VMEM((layers, width // LANES, rows + 16, LANES), f32),
        pltpu.VMEM((layers, width // LANES, rows + 16, LANES), f32),
        pltpu.VMEM((layers, rows, width), f32),
        pltpu.VMEM((chans, rows, width), f32),
        pltpu.VMEM((rows, width), jnp.int32),
        pltpu.VMEM((rows, width), f32),
        pltpu.SMEM(power_levels.shape, f32),
        pltpu.VMEM((chans, width), jnp.int32),
        pltpu.VMEM((chans, width), f32),
        pltpu.VMEM((chans, width), f32),
        pltpu.VMEM((2, 2, layers, width), f32),
        pltpu.VMEM((2, 2, packed, LANES), f32),
        pltpu.VMEM((2, 2, layers, width), f32),
        pltpu.VMEM((2, 2, packed, LANES), f32),
        pltpu.VMEM((totals, width), f32),
        pltpu.VMEM((n_flow - 1, totals, width), f32),
        pltpu.SemaphoreType.DMA((4, width // LANES)),
        pltpu.SemaphoreType.DMA((4, 4)),
        pltpu.SemaphoreType.DMA((4,)),
        pltpu.SemaphoreType.DMA((2, 4)),
        pltpu.SemaphoreType.DMA((2, 4)),
        pltpu.SemaphoreType.DMA((n_flow - 1,)),
        pltpu.SemaphoreType.DMA((n_flow - 1,)),
    ]
    cells = layers * rows * width
    limit = 57 * 1024 * 1024
    solid, within, ends = pl.pallas_call(
        functools.partial(kernel, n_flow, n_cross),
        out_shape=(
            pltpu.VMEM((layers, rows, width), f32),
            pltpu.VMEM((chans, rows, width), f32),
            pltpu.VMEM((2, chans, width), f32),
        ),
        in_specs=[pl.BlockSpec(memory_space=pltpu.HBM)] * 8,
        out_specs=(pl.BlockSpec(memory_space=pltpu.VMEM),) * 3,
        scratch_shapes=scratch,
        compiler_params=pltpu.CompilerParams(
            collective_id=0, has_side_effects=True, vmem_limit_bytes=limit
        ),
        cost_estimate=pl.CostEstimate(
            flops=40 * cells, bytes_accessed=11 * cells, transcendentals=0
        ),
    )(
        solid_temp, conductance, coolant, power_index, power_levels, channel_mask, inlet, flow_gain
    )
    return pl.pallas_call(
        finish,
        out_shape=(
            jax.ShapeDtypeStruct((layers, rows, width), f32),
            jax.ShapeDtypeStruct((chans, rows, width), f32),
        ),
        in_specs=[pl.BlockSpec(memory_space=pltpu.VMEM)] * 3,
        out_specs=(pl.BlockSpec(memory_space=pltpu.HBM),) * 2,
        scratch_shapes=[
            pltpu.VMEM((chans, rows, width), f32),
            pltpu.SemaphoreType.DMA((layers,)),
            pltpu.SemaphoreType.DMA((chans,)),
        ],
        compiler_params=pltpu.CompilerParams(vmem_limit_bytes=16 * 1024 * 1024),
        cost_estimate=pl.CostEstimate(flops=cells, bytes_accessed=6 * cells, transcendentals=0),
    )(solid, within, ends)


def solution(mesh):
    return jax.shard_map(
        shards,
        mesh=mesh,
        in_specs=(
            P(None, "flow", "cross"),
            P(None, "flow", "cross"),
            P(None, "flow", "cross"),
            P("flow", "cross"),
            P(),
            P(None, "cross"),
            P(None, "cross"),
            P(None, "cross"),
        ),
        out_specs=(P(None, "flow", "cross"), P(None, "flow", "cross")),
        check_vma=False,
    )
```
